32 devices in a mesh: alpha: 8 (over y, x, core), beta: 4 (over z).
Axes of the slice: x: 2, y: 2, z: 4, core: 2. Of those that a mesh axis runs over, the one named last changes fastest.
Arguments:
- coefficients: float32 [6144, 3072], P('alpha', 'beta'), may hold values from -6 to 6
- beta_blocks: float32 [8, 3, 384, 384], P('beta'), may hold values from -0.1875 to 0.1875
- alpha_blocks: float32 [16, 3, 384, 384], P('alpha'), may hold values from -0.1875 to 0.1875
- beta_links: int32 [8, 3], P('beta'), may hold values from 0 to 7, as said below
- alpha_links: int32 [16, 3], P('alpha'), may hold values from 0 to 15, as said below
- beta_count: int32 [8], P('beta'), may hold values from 1 to 3, as said below
- alpha_count: int32 [16], P('alpha'), may hold values from 1 to 3, as said below
Outputs:
- sigma_slab: float32 [6144, 3072], P('alpha', 'beta')
The draws below stay inside these ranges and needn't reach their ends.
Inputs may be any that keep to these rules, and one draw needn't show every extreme that they name: `beta_links`: each row lists 3 distinct beta groups whose cyclic distance from the row's own group is at most 2. `alpha_links`: each row lists 3 distinct alpha groups whose cyclic distance from the row's own group is at most 2. `beta_count`: some group uses all 3 couplings. `alpha_count`: some group uses all 3 couplings.
All inputs are finite; a program needn't handle non-finite values.
Results may differ from the reference program's by a relative error of at most 0.0003.
Values sent between devices are 32-bit elements; how exact they have to be, the bound alone decides.
No kernel may reach another device: no remote copies, remote signals or barrier semaphores. Data moves between devices by JAX's collectives and lax.ppermute only.
A program may use at most 128 MiB of HBM per device.

```python
import jax
import jax.numpy as jnp
from jax import lax

G = 384
REACH = 2
LIST = 3
GROUPS_A = 16
GROUPS_B = 8
SA = 6144
SB = 3072


def link_table(key, groups):
    row_keys = jax.random.split(key, groups)
    orders = jax.vmap(lambda one_key: jax.random.permutation(one_key, 2 * REACH + 1))(row_keys)
    offsets = orders[:, :LIST] - REACH
    return ((jnp.arange(groups)[:, None] + offsets) % groups).astype(jnp.int32)


def count_table(key, groups):
    counts = jax.random.randint(key, (groups,), 1, LIST + 1)
    position = jax.random.randint(jax.random.fold_in(key, 5), (), 0, groups)
    return counts.at[position].set(LIST).astype(jnp.int32)


def draw_beta_links(key, part):
    return link_table(jax.random.fold_in(key, 11), GROUPS_B)


def draw_alpha_links(key, part):
    return link_table(jax.random.fold_in(key, 12), GROUPS_A)


def draw_beta_count(key, part):
    return count_table(jax.random.fold_in(key, 13), GROUPS_B)


def draw_alpha_count(key, part):
    return count_table(jax.random.fold_in(key, 14), GROUPS_A)


def shard_levels(stream_key, dims, cuts, least, largest):
    loudness, own = 1.0, jax.random.fold_in(stream_key, 6)
    for axis_at, parts in cuts:
        draws = jnp.exp(jax.random.uniform(jax.random.fold_in(own, axis_at), (parts,), jnp.float32, least / len(cuts), largest / len(cuts)))
        loudness = loudness * jnp.repeat(draws, dims[axis_at] // parts).reshape([-1 if axis == axis_at else 1 for axis in range(len(dims))])
    return loudness


def bell_draw(own_key, shape, width, reach, cuts=(), held_as=jnp.bfloat16):
    values = jax.random.normal(own_key, shape, jnp.float32) * width
    if len(cuts) > 0:
        values = shard_levels(own_key, shape, cuts, -0.22, 0.18) * values
    return jnp.clip(values, min=-reach, max=reach).astype(held_as)


def setup_inputs(seed: int = 0) -> dict:
    keys = jax.random.split(jax.random.key(seed), 8)
    return {
        "coefficients": bell_draw(keys[0], (SA, SB), 1.0, 6.0, ((0, 8), (1, 4)), jnp.float32),
        "beta_blocks": bell_draw(keys[1], (GROUPS_B, LIST, G, G), (G * LIST) ** -0.5, 0.1875, ((0, 4),), jnp.float32),
        "alpha_blocks": bell_draw(keys[2], (GROUPS_A, LIST, G, G), (G * LIST) ** -0.5, 0.1875, ((0, 8),), jnp.float32),
        "beta_links": draw_beta_links(jax.random.fold_in(keys[7], 71), 0),
        "alpha_links": draw_alpha_links(jax.random.fold_in(keys[7], 71), 0),
        "beta_count": draw_beta_count(jax.random.fold_in(keys[7], 71), 0),
        "alpha_count": draw_alpha_count(jax.random.fold_in(keys[7], 71), 0),
    }


def beta_part_of(coefficients, beta_blocks, beta_links, beta_count):
    def one_group(group):
        def accumulate(position, running):
            source = beta_links[group, position].astype(jnp.int32)
            columns = lax.dynamic_slice_in_dim(coefficients, (source * G).astype(jnp.int32), G, 1)
            return running + jnp.dot(columns, beta_blocks[group, position], precision=lax.Precision.HIGHEST, preferred_element_type=jnp.float32)
        start = jnp.zeros((coefficients.shape[0], G), coefficients.dtype)
        return lax.fori_loop(0, beta_count[group], accumulate, start)
    pieces = lax.map(one_group, jnp.arange(GROUPS_B, dtype=jnp.int32))
    return jnp.transpose(pieces, (1, 0, 2)).reshape(coefficients.shape[0], GROUPS_B * G)


def alpha_part_of(coefficients, alpha_blocks, alpha_links, alpha_count):
    def one_group(group):
        def accumulate(position, running):
            source = alpha_links[group, position].astype(jnp.int32)
            rows = lax.dynamic_slice_in_dim(coefficients, (source * G).astype(jnp.int32), G, 0)
            return running + jnp.dot(alpha_blocks[group, position], rows, precision=lax.Precision.HIGHEST, preferred_element_type=jnp.float32)
        start = jnp.zeros((G, coefficients.shape[1]), coefficients.dtype)
        return lax.fori_loop(0, alpha_count[group], accumulate, start)
    pieces = lax.map(one_group, jnp.arange(GROUPS_A, dtype=jnp.int32))
    return pieces.reshape(GROUPS_A * G, coefficients.shape[1])


def reference(coefficients, beta_blocks, alpha_blocks, beta_links, alpha_links, beta_count, alpha_count):
    beta_part = beta_part_of(coefficients, beta_blocks, beta_links, beta_count)
    alpha_part = alpha_part_of(coefficients, alpha_blocks, alpha_links, alpha_count)
    return beta_part + alpha_part
```

```python
import functools

import jax
import jax.numpy as jnp
from jax import lax
from jax.experimental import pallas as pl
from jax.experimental.pallas import tpu as pltpu
from jax.sharding import PartitionSpec as P

VMEM_LIMIT = 56 * 1024 * 1024


def halves(x):
    high = x.astype(jnp.bfloat16)
    low = (x - high.astype(jnp.float32)).astype(jnp.bfloat16)
    return high, low


def product(left, right):
    lh, ll = halves(left)
    rh, rl = halves(right)
    dot = functools.partial(jnp.dot, preferred_element_type=jnp.float32)
    return dot(lh, rh) + (dot(lh, rl) + dot(ll, rh))


def place(links, count, my_index, owners):
    per, listed = links.shape
    slot = (links - my_index * per + per) % (owners * per)
    return jnp.where(jnp.arange(listed)[None, :] < count[:, None], slot, -1).reshape(-1)


def add_rows(slots, base, at, tile, blocks, out, listed, group, per):
    def step(l, carry):
        slot = slots[at * listed + l]

        @pl.when((slot >= base) & (slot < base + per))
        def _():
            rows = pl.ds(pl.multiple_of((slot - base) * group, group), group)
            out[...] += product(blocks[0, l], tile[rows, :])

        return carry

    lax.fori_loop(0, listed, step, 0)


def add_columns(slots, offset, base, tile, blocks, out, listed, group, per):
    for c in range(per):

        def step(l, carry, c=c):
            slot = slots[offset + c * listed + l]

            @pl.when((slot >= base) & (slot < base + per))
            def _():
                columns = pl.ds(pl.multiple_of((slot - base) * group, group), group)
                out[:, c * group : (c + 1) * group] += product(tile[:, columns], blocks[c, l])

            return carry

        lax.fori_loop(0, listed, step, 0)


def own_kernel(slots, tile, tile_rows, ablocks, bblocks, out):
    per, listed, group, _ = bblocks.shape
    out[...] = jnp.zeros_like(out)
    add_rows(slots, per, pl.program_id(0), tile, ablocks, out, listed, group, per)
    add_columns(slots, per * listed, per, tile_rows, bblocks, out, listed, group, per)


def alpha_kernel(per, slots, running, behind, ahead, ablocks, out):
    _, listed, group, _ = ablocks.shape
    out[...] = running[...]
    for base, tile in ((0, behind), (2 * per, ahead)):
        add_rows(slots, base, pl.program_id(0), tile, ablocks, out, listed, group, per)


def beta_kernel(slots, running, behind, ahead, bblocks, out):
    per, listed, group, _ = bblocks.shape
    out[...] = running[...]
    for base, tile in ((0, behind), (2 * per, ahead)):
        add_columns(slots, per * listed, base, tile, bblocks, out, listed, group, per)


def call(kernel, grid, in_specs, out_spec, shape, flops, name, aliases):
    return pl.pallas_call(
        kernel,
        grid_spec=pltpu.PrefetchScalarGridSpec(
            num_scalar_prefetch=1, grid=(grid,), in_specs=in_specs, out_specs=out_spec
        ),
        out_shape=jax.ShapeDtypeStruct(shape, jnp.float32),
        input_output_aliases=aliases,
        compiler_params=pltpu.CompilerParams(vmem_limit_bytes=VMEM_LIMIT),
        cost_estimate=pl.CostEstimate(flops=flops, bytes_accessed=16 * 1024 * 1024, transcendentals=0),
        name=name,
    )


def on_device(c, bblocks, ablocks, blinks, alinks, bcount, acount):
    rows, columns = c.shape
    per, listed, group, _ = ablocks.shape
    na, nb = lax.axis_size("alpha"), lax.axis_size("beta")

    def shift(x, axis, n, by):
        return lax.ppermute(x, axis, [(i, (i + by) % n) for i in range(n)])

    b_behind = shift(c, "beta", nb, 1)
    b_ahead = shift(c, "beta", nb, -1)
    a_behind = shift(c, "alpha", na, 1)
    a_ahead = shift(c, "alpha", na, -1)

    slots = jnp.concatenate(
        [
            place(alinks, acount, lax.axis_index("alpha"), na),
            place(blinks, bcount, lax.axis_index("beta"), nb),
        ]
    )

    def whole(*shape):
        return pl.BlockSpec(shape, lambda i, s: (0,) * len(shape))

    def by_rows(n):
        return pl.BlockSpec((n, columns), lambda i, s: (i, 0))

    group_blocks = pl.BlockSpec((1, listed, group, group), lambda i, s: (i, 0, 0, 0))
    flops = 2 * rows * group * group * 3 * 3
    own = call(
        own_kernel, per,
        [whole(rows, columns), by_rows(group), group_blocks, whole(*bblocks.shape)],
        by_rows(group), c.shape, 2 * flops, "own_groups", {},
    )(slots, c, c, ablocks, bblocks)
    with_alpha = call(
        functools.partial(alpha_kernel, per), per,
        [by_rows(group), whole(rows, columns), whole(rows, columns), group_blocks],
        by_rows(group), c.shape, flops, "alpha_neighbours", {1: 0},
    )(slots, own, a_behind, a_ahead, ablocks)
    chunks = 4
    return call(
        beta_kernel, chunks,
        [by_rows(rows // chunks)] * 3 + [whole(*bblocks.shape)],
        by_rows(rows // chunks), c.shape, flops, "beta_neighbours", {1: 0},
    )(slots, with_alpha, b_behind, b_ahead, bblocks)


def solution(mesh):
    in_specs = (
        P("alpha", "beta"),
        P("beta", None, None, None),
        P("alpha", None, None, None),
        P("beta", None),
        P("alpha", None),
        P("beta"),
        P("alpha"),
    )
    return jax.shard_map(
        on_device, mesh=mesh, in_specs=in_specs, out_specs=P("alpha", "beta"), check_vma=False
    )
```

```python
import functools

import jax
import jax.numpy as jnp
from jax import lax
from jax.experimental import pallas as pl
from jax.experimental.pallas import tpu as pltpu
from jax.sharding import PartitionSpec as P

VMEM_LIMIT = 56 * 1024 * 1024


def halves(x):
    high = x.astype(jnp.bfloat16)
    low = (x - high.astype(jnp.float32)).astype(jnp.bfloat16)
    return high, low


def split(x, high, low):
    high[...], low[...] = halves(x)


def add_product(out, left, right):
    (lh, ll), (rh, rl) = left, right
    dot = functools.partial(jnp.dot, preferred_element_type=jnp.float32)
    out[...] += dot(lh[...], rh[...]) + (dot(lh[...], rl[...]) + dot(ll[...], rh[...]))


def at(index, size):
    return pl.ds(pl.multiple_of(index * size, size), size)


OWN, UNUSED = 0, 13
EVEN, ODD, ENDS = range(3)
BEHIND, AHEAD = range(2)
NEAR, FAR = range(2)


def kind_of(pair, side, rank):
    return 1 + 4 * pair + 2 * side + rank


def mask_of(pairs=(EVEN, ODD, ENDS), sides=(BEHIND, AHEAD), ranks=(NEAR, FAR)):
    return sum(1 << kind_of(p, s, r) for p in pairs for s in sides for r in ranks)


def tables_kernel(owners, blinks, alinks, bcount, acount, slots, code):
    per, listed = blinks.shape
    (yn, zn), yi, zi = owners, lax.axis_index("alpha"), lax.axis_index("beta")
    first, last, even = zi == 0, zi == zn - 1, lax.rem(zi, 2) == 0
    pair_behind = jnp.where(first, ENDS, jnp.where(even, ODD, EVEN))
    pair_ahead = jnp.where(last, ENDS, jnp.where(even, EVEN, ODD))

    def where(links, count, g, l, index, n):
        slot = lax.rem(links[g, l] - index * per + per + n * per, n * per)
        return jnp.where(l < count[g], slot, -1)

    nb = fb = na = fa = jnp.int32(0)
    for g in range(per):
        for l in range(listed):
            slots[g * listed + l] = where(alinks, acount, g, l, yi, yn)
            slot = where(blinks, bcount, g, l, zi, zn)
            nb |= (slot == per - 1).astype(jnp.int32)
            fb |= (slot == per - 2).astype(jnp.int32)
            na |= (slot == 2 * per).astype(jnp.int32)
            fa |= (slot == 2 * per + 1).astype(jnp.int32)
            behind = kind_of(pair_behind, BEHIND, jnp.where(slot == per - 1, NEAR, FAR))
            ahead = kind_of(pair_ahead, AHEAD, jnp.where(slot == 2 * per, NEAR, FAR))
            kind = jnp.where(slot < per, behind, jnp.where(slot < 2 * per, OWN, ahead))
            kind = jnp.where(slot < 0, UNUSED, kind)
            slots[(per + g) * listed + l] = kind * per + lax.rem(slot + per, per)
    behind, ahead = nb + fb, na + fa
    climb = jnp.where(first, 0, behind >> 1)
    descend = jnp.where(last, 0, ahead >> 1)
    over = jnp.where(first, behind, 0)
    back = jnp.where(last, ahead, 0)
    code[0] = climb + (descend << 6) + (over << 12) + (back << 14) + (nb << 16) + (na << 17)


def plan_kernel(per, owners, *refs):
    *codes, index, chosen = refs
    total = jnp.int32(0)
    for code in codes:
        total += code[0] & 0xFFFF
    climb, descend = (total & 63) > 0, ((total >> 6) & 63) > 0
    over, back = ((total >> 12) & 3) == 2, ((total >> 14) & 3) == 2
    full = (climb & back) | (descend & over) | (over & back)
    some = climb | descend | over | back
    index[0] = jnp.where(full, 4, jnp.where(over, 2, jnp.where(back, 3, some.astype(jnp.int32))))
    to_ahead = jnp.where(((codes[owners - 1][0] >> 16) & 1) == 1, per - 1, per - 2)
    to_behind = jnp.where(((codes[1][0] >> 17) & 1) == 1, 0, 1)
    even = lax.rem(lax.axis_index("beta"), 2) == 0
    chosen[0] = to_ahead
    chosen[1] = to_behind
    chosen[2] = jnp.where(even, to_behind, to_ahead)
    chosen[3] = jnp.where(even, 1, per - 2)


def pick_kernel(chosen, *refs):
    for source, target in zip(refs[: len(refs) // 2], refs[len(refs) // 2 :], strict=True):
        target[...] = source[...]


def own_kernel(slots, tile, tile_rows, ablocks, bblocks, out, high, low, lh, ll, rh, rl):
    per, listed, group, _ = bblocks.shape
    row = pl.program_id(0)
    out[...] = jnp.zeros_like(out)

    def step(t, carry):
        g, l = t // listed, lax.rem(t, listed)
        a_slot, b_slot = slots[row * listed + l], slots[per * listed + t]

        @pl.when(row == 0)
        def _():
            split(bblocks[g, l], high.at[g, l], low.at[g, l])

        @pl.when((a_slot >= per) & (a_slot < 2 * per))
        def _():
            split(ablocks[0, l], lh, ll)
            split(tile[at(a_slot - per, group), at(g, group)], rh, rl)
            add_product(out.at[:, at(g, group)], (lh, ll), (rh, rl))

        @pl.when(lax.div(b_slot, per) == OWN)
        def _():
            split(tile_rows[:, at(b_slot, group)], lh, ll)
            add_product(out.at[:, at(g, group)], (lh, ll), (high.at[g, l], low.at[g, l]))

        return carry

    lax.fori_loop(0, per * listed, step, 0)


def alpha_kernel(slots, running, behind, ahead, ablocks, out, lh, ll, rh, rl):
    _, listed, group, _ = ablocks.shape
    per = behind.shape[0] // group
    row = pl.program_id(0)
    out[...] = running[...]

    def step(t, carry):
        l, g = t // per, lax.rem(t, per)
        slot = slots[row * listed + l]
        below, above = (slot >= 0) & (slot < per), slot >= 2 * per
        for inside, tile, base in ((below, behind, 0), (above, ahead, 2 * per)):

            @pl.when(inside)
            def _(tile=tile, base=base):
                split(tile[at(slot - base, group), at(g, group)], rh, rl)

        @pl.when((below | above) & (g == 0))
        def _():
            split(ablocks[0, l], lh, ll)

        @pl.when(below | above)
        def _():
            add_product(out.at[:, at(g, group)], (lh, ll), (rh, rl))

        return carry

    lax.fori_loop(0, per * listed, step, 0)


def beta_kernel(masks, slots, running, *refs):
    *buffers, high, low, out, lh, ll = refs
    per, listed, group, _ = high.shape
    out[...] = running[...]

    def step(t, carry):
        g, l = t // listed, lax.rem(t, listed)
        slot = slots[per * listed + t]
        hits = []
        for mask, tile in zip(masks, buffers, strict=True):
            hits.append(((mask >> lax.div(slot, per)) & 1) == 1)

            @pl.when(hits[-1])
            def _(tile=tile):
                part = tile[...] if tile.shape[1] == group else tile[:, at(lax.rem(slot, per), group)]
                split(part, lh, ll)

        @pl.when(functools.reduce(jnp.logical_or, hits))
        def _():
            add_product(out.at[:, at(g, group)], (lh, ll), (high.at[g, l], low.at[g, l]))

        return carry

    lax.fori_loop(0, per * listed, step, 0)


def call(kernel, grid, in_specs, out_spec, shape, scratch, flops, name, aliases, vmem=VMEM_LIMIT):
    return pl.pallas_call(
        kernel,
        grid_spec=pltpu.PrefetchScalarGridSpec(
            num_scalar_prefetch=1, grid=(grid,), in_specs=in_specs, out_specs=out_spec,
            scratch_shapes=[pltpu.VMEM(x, jnp.bfloat16) for x in scratch],
        ),
        out_shape=shape,
        input_output_aliases=aliases,
        compiler_params=pltpu.CompilerParams(vmem_limit_bytes=vmem),
        cost_estimate=pl.CostEstimate(flops=flops, bytes_accessed=16 * 1024 * 1024, transcendentals=0),
        name=name,
    )


def on_device(c, bblocks, ablocks, blinks, alinks, bcount, acount):
    rows, columns = c.shape
    per, listed, group, _ = ablocks.shape
    na, nb = lax.axis_size("alpha"), lax.axis_size("beta")
    smem = pl.BlockSpec(memory_space=pltpu.SMEM)
    slots, code = pl.pallas_call(
        functools.partial(tables_kernel, (na, nb)),
        in_specs=[smem] * 4,
        out_specs=[smem] * 2,
        out_shape=[jax.ShapeDtypeStruct((2 * per * listed,), jnp.int32), jax.ShapeDtypeStruct((1,), jnp.int32)],
        name="tables",
    )(blinks, alinks, bcount, acount)

    codes = [code] + [
        lax.ppermute(code, "beta", [(i, (i + by) % nb) for i in range(nb)]) for by in range(1, nb)
    ]
    index, chosen = pl.pallas_call(
        functools.partial(plan_kernel, per, nb),
        in_specs=[smem] * nb,
        out_specs=[smem] * 2,
        out_shape=[jax.ShapeDtypeStruct((1,), jnp.int32), jax.ShapeDtypeStruct((4,), jnp.int32)],
        name="plan",
    )(*codes)

    def whole(*shape):
        return pl.BlockSpec(shape, lambda i, s: (0,) * len(shape))

    def by_rows(n, width=columns):
        return pl.BlockSpec((n, width), lambda i, s: (i, 0))

    group_blocks = pl.BlockSpec((1, listed, group, group), lambda i, s: (i, 0, 0, 0))
    slab = whole(rows, columns)
    result = jax.ShapeDtypeStruct(c.shape, jnp.float32)
    half = jax.ShapeDtypeStruct(bblocks.shape, jnp.bfloat16)
    flops = 2 * rows * group * group * 3 * 3
    chunks = 2
    ring = [(i, (i + 1) % nb) for i in range(nb)]
    counter = [(j, i) for i, j in ring]
    even_pairs = [p for i in range(0, nb - 1, 2) for p in ((i, i + 1), (i + 1, i))]
    odd_pairs = [p for i in range(1, nb - 1, 2) for p in ((i, i + 1), (i + 1, i))]
    end_pairs = [(0, nb - 1), (nb - 1, 0)]

    def pick(chosen, c, *which):
        half_rows = rows // 2
        return pl.pallas_call(
            pick_kernel,
            grid_spec=pltpu.PrefetchScalarGridSpec(
                num_scalar_prefetch=1,
                grid=(2,),
                in_specs=[pl.BlockSpec((half_rows, group), lambda i, s, w=w: (i, s[w])) for w in which],
                out_specs=[by_rows(half_rows, group) for w in which],
            ),
            out_shape=[jax.ShapeDtypeStruct((rows, group), c.dtype) for w in which],
            name="pick",
        )(chosen, *[c for w in which])

    def own_groups(slots, c, ablocks, bblocks):
        return call(
            own_kernel, per,
            [slab, by_rows(group), group_blocks, whole(*bblocks.shape)],
            [by_rows(group), whole(*bblocks.shape), whole(*bblocks.shape)], [result, half, half],
            [(group, group)] * 4, 2 * flops, "own_groups", {},
        )(slots, c, c, ablocks, bblocks)

    def alpha_groups(slots, running, behind, ahead, ablocks):
        return call(
            alpha_kernel, per, [by_rows(group), slab, slab, group_blocks],
            by_rows(group), result, [(group, group)] * 4, 2 * flops, "alpha_groups", {1: 0},
        )(slots, running, behind, ahead, ablocks)

    def beta_groups(slots, running, high, low, arrived):
        def rows_of(x):
            return by_rows(rows // chunks, x.shape[1])

        return call(
            functools.partial(beta_kernel, [mask for mask, _ in arrived]), chunks,
            [rows_of(running)] + [rows_of(x) for _, x in arrived] + [whole(*bblocks.shape)] * 2,
            rows_of(running), result, [(rows // chunks, group)] * 2, flops, "beta_groups", {1: 0}, 20 * 1024 * 1024,
        )(slots, running, *[x for _, x in arrived], high, low)

    def branch(*sends):
        def body(c, ablocks, bblocks, slots, chosen):
            which = [what for _, _, what in sends if what is not None]
            picked = dict(zip(which, pick(chosen, c, *which), strict=True)) if which else {}
            arrived = []
            for pairs, mask, what in sends:
                arrived.append((mask, lax.ppermute(c if what is None else picked[what], "beta", pairs)))
            a_behind = lax.ppermute(c, "alpha", [(i, (i + 1) % na) for i in range(na)])
            a_ahead = lax.ppermute(c, "alpha", [(i, (i - 1) % na) for i in range(na)])
            running, high, low = own_groups(slots, c, ablocks, bblocks)
            running = alpha_groups(slots, running, a_behind, a_ahead, ablocks)
            running = beta_groups(slots, running, high, low, arrived[:1])
            return beta_groups(slots, running, high, low, arrived[1:])

        return body

    tile, to_ahead, to_behind, to_odd, far_odd = None, 0, 1, 2, 3
    below, above = mask_of(sides=(BEHIND,)), mask_of(sides=(AHEAD,))
    mixed = mask_of((ENDS,)) | mask_of((ODD,), ranks=(NEAR,))
    branches = [
        branch((ring, below, to_ahead), (counter, above, to_behind)),
        branch((even_pairs, mask_of((EVEN,)), tile), (odd_pairs + end_pairs, mixed, to_odd), (odd_pairs, mask_of((ODD,), ranks=(FAR,)), far_odd)),
        branch((ring, below, tile), (counter, above, to_behind)),
        branch((counter, above, tile), (ring, below, to_ahead)),
        branch((ring, below, tile), (counter, above, tile)),
    ]
    return lax.switch(index[0], branches, c, ablocks, bblocks, slots, chosen)


def solution(mesh):
    in_specs = (
        P("alpha", "beta"),
        P("beta", None, None, None),
        P("alpha", None, None, None),
        P("beta", None),
        P("alpha", None),
        P("beta"),
        P("alpha"),
    )
    return jax.shard_map(
        on_device, mesh=mesh, in_specs=in_specs, out_specs=P("alpha", "beta"), check_vma=False
    )
```

```python
import functools

import jax
import jax.numpy as jnp
from jax import lax
from jax.experimental import pallas as pl
from jax.experimental.pallas import tpu as pltpu
from jax.sharding import PartitionSpec as P

VMEM_LIMIT = 56 * 1024 * 1024


def halves(x):
    high = x.astype(jnp.bfloat16)
    low = (x - high.astype(jnp.float32)).astype(jnp.bfloat16)
    return high, low


def split(x, high, low):
    high[...], low[...] = halves(x)


def add_product(out, left, right):
    (lh, ll), (rh, rl) = left, right
    dot = functools.partial(jnp.dot, preferred_element_type=jnp.float32)
    out[...] += dot(lh[...], rh[...]) + (dot(lh[...], rl[...]) + dot(ll[...], rh[...]))


def at(index, size):
    return pl.ds(pl.multiple_of(index * size, size), size)


OWN, UNUSED = 0, 13
EVEN, ODD, ENDS = range(3)
BEHIND, AHEAD = range(2)
NEAR, FAR = range(2)


def kind_of(pair, side, rank):
    return 1 + 4 * pair + 2 * side + rank


def mask_of(pairs=(EVEN, ODD, ENDS), sides=(BEHIND, AHEAD), ranks=(NEAR, FAR)):
    return sum(1 << kind_of(p, s, r) for p in pairs for s in sides for r in ranks)


def tables_kernel(owners, blinks, alinks, bcount, acount, slots, code):
    per, listed = blinks.shape
    (yn, zn), yi, zi = owners, lax.axis_index("alpha"), lax.axis_index("beta")
    first, last, even = zi == 0, zi == zn - 1, lax.rem(zi, 2) == 0
    pair_behind = jnp.where(first, ENDS, jnp.where(even, ODD, EVEN))
    pair_ahead = jnp.where(last, ENDS, jnp.where(even, EVEN, ODD))

    def where(links, count, g, l, index, n):
        slot = lax.rem(links[g, l] - index * per + per + n * per, n * per)
        return jnp.where(l < count[g], slot, -1)

    nb = fb = na = fa = jnp.int32(0)
    for g in range(per):
        for l in range(listed):
            slots[g * listed + l] = where(alinks, acount, g, l, yi, yn)
            slot = where(blinks, bcount, g, l, zi, zn)
            nb |= (slot == per - 1).astype(jnp.int32)
            fb |= (slot == per - 2).astype(jnp.int32)
            na |= (slot == 2 * per).astype(jnp.int32)
            fa |= (slot == 2 * per + 1).astype(jnp.int32)
            behind = kind_of(pair_behind, BEHIND, jnp.where(slot == per - 1, NEAR, FAR))
            ahead = kind_of(pair_ahead, AHEAD, jnp.where(slot == 2 * per, NEAR, FAR))
            kind = jnp.where(slot < per, behind, jnp.where(slot < 2 * per, OWN, ahead))
            kind = jnp.where(slot < 0, UNUSED, kind)
            slots[(per + g) * listed + l] = kind * per + lax.rem(slot + per, per)
    behind, ahead = nb + fb, na + fa
    climb = jnp.where(first, 0, behind >> 1)
    descend = jnp.where(last, 0, ahead >> 1)
    over = jnp.where(first, behind, 0)
    back = jnp.where(last, ahead, 0)
    code[0] = code[1] = climb + (descend << 6) + (over << 12) + (back << 14) + (nb << 16) + (na << 17)


def pick_kernel(chosen, *refs):
    for source, target in zip(refs[: len(refs) // 2], refs[len(refs) // 2 :], strict=True):
        target[...] = source[...]


def own_kernel(slots, tile, tile_rows, ablocks, bblocks, out, high, low, lh, ll, rh, rl):
    per, listed, group, _ = bblocks.shape
    row = pl.program_id(0)
    out[...] = jnp.zeros_like(out)

    def step(t, carry):
        g, l = t // listed, lax.rem(t, listed)
        a_slot, b_slot = slots[row * listed + l], slots[per * listed + t]

        @pl.when(row == 0)
        def _():
            split(bblocks[g, l], high.at[g, l], low.at[g, l])

        @pl.when((a_slot >= per) & (a_slot < 2 * per))
        def _():
            split(ablocks[0, l], lh, ll)
            split(tile[at(a_slot - per, group), at(g, group)], rh, rl)
            add_product(out.at[:, at(g, group)], (lh, ll), (rh, rl))

        @pl.when(lax.div(b_slot, per) == OWN)
        def _():
            split(tile_rows[:, at(b_slot, group)], lh, ll)
            add_product(out.at[:, at(g, group)], (lh, ll), (high.at[g, l], low.at[g, l]))

        return carry

    lax.fori_loop(0, per * listed, step, 0)


def alpha_kernel(slots, running, behind, ahead, ablocks, out, lh, ll, rh, rl):
    _, listed, group, _ = ablocks.shape
    per = behind.shape[0] // group
    row = pl.program_id(0)
    out[...] = running[...]

    def step(t, carry):
        l, g = t // per, lax.rem(t, per)
        slot = slots[row * listed + l]
        below, above = (slot >= 0) & (slot < per), slot >= 2 * per
        for inside, tile, base in ((below, behind, 0), (above, ahead, 2 * per)):

            @pl.when(inside)
            def _(tile=tile, base=base):
                split(tile[at(slot - base, group), at(g, group)], rh, rl)

        @pl.when((below | above) & (g == 0))
        def _():
            split(ablocks[0, l], lh, ll)

        @pl.when(below | above)
        def _():
            add_product(out.at[:, at(g, group)], (lh, ll), (rh, rl))

        return carry

    lax.fori_loop(0, per * listed, step, 0)


def beta_kernel(masks, slots, running, *refs):
    *buffers, high, low, out, lh, ll = refs
    per, listed, group, _ = high.shape
    out[...] = running[...]

    def step(t, carry):
        g, l = t // listed, lax.rem(t, listed)
        slot = slots[per * listed + t]
        hits = []
        for mask, tile in zip(masks, buffers, strict=True):
            hits.append(((mask >> lax.div(slot, per)) & 1) == 1)

            @pl.when(hits[-1])
            def _(tile=tile):
                part = tile[...] if tile.shape[1] == group else tile[:, at(lax.rem(slot, per), group)]
                split(part, lh, ll)

        @pl.when(functools.reduce(jnp.logical_or, hits))
        def _():
            add_product(out.at[:, at(g, group)], (lh, ll), (high.at[g, l], low.at[g, l]))

        return carry

    lax.fori_loop(0, per * listed, step, 0)


def call(kernel, grid, in_specs, out_spec, shape, scratch, flops, name, aliases, vmem=VMEM_LIMIT):
    return pl.pallas_call(
        kernel,
        grid_spec=pltpu.PrefetchScalarGridSpec(
            num_scalar_prefetch=1, grid=(grid,), in_specs=in_specs, out_specs=out_spec,
            scratch_shapes=[pltpu.VMEM(x, jnp.bfloat16) for x in scratch],
        ),
        out_shape=shape,
        input_output_aliases=aliases,
        compiler_params=pltpu.CompilerParams(vmem_limit_bytes=vmem),
        cost_estimate=pl.CostEstimate(flops=flops, bytes_accessed=16 * 1024 * 1024, transcendentals=0),
        name=name,
    )


def on_device(c, bblocks, ablocks, blinks, alinks, bcount, acount):
    rows, columns = c.shape
    per, listed, group, _ = ablocks.shape
    na, nb = lax.axis_size("alpha"), lax.axis_size("beta")
    smem = pl.BlockSpec(memory_space=pltpu.SMEM)
    slots, code = pl.pallas_call(
        functools.partial(tables_kernel, (na, nb)),
        in_specs=[smem] * 4,
        out_specs=[smem] * 2,
        out_shape=[jax.ShapeDtypeStruct((2 * per * listed,), jnp.int32), jax.ShapeDtypeStruct((2,), jnp.int32)],
        name="tables",
    )(blinks, alinks, bcount, acount)

    codes = [code] + [
        lax.ppermute(code, "beta", [(i, (i + by) % nb) for i in range(nb)]) for by in range(1, nb)
    ]
    z = lax.axis_index("beta")
    even = z % 2 == 0
    near_odd = lax.dynamic_slice_in_dim(c, jnp.where(even, 0, per - 1) * group, group, 1)
    *codes, near_odd = lax.optimization_barrier((*codes, near_odd))
    total = functools.reduce(lambda x, y: x + y, [x & 0xFFFF for x in codes])
    climb, descend = (total & 0x3F) > 0, (total & 0xFC0) > 0
    over, back = (total & 0x3000) == 0x2000, (total & 0xC000) == 0x8000
    full = (climb & back) | (descend & over) | (over & back)
    some = (climb | descend).astype(jnp.int32)
    index = jnp.where(full, 4, jnp.where(over, 2, jnp.where(back, 3, some)))
    to_ahead = jnp.where((codes[nb - 1] & 0x10000) > 0, per - 1, per - 2)
    to_behind = jnp.where((codes[1] & 0x20000) > 0, 0, 1)
    far_odd = jnp.where(even, 1, per - 2)
    to_end = jnp.where(even, to_behind, to_ahead)
    chosen = jnp.stack([to_ahead, to_behind, jnp.where((z == 0) | (z == nb - 1), to_end, far_odd)])[:, 0]

    def whole(*shape):
        return pl.BlockSpec(shape, lambda i, s: (0,) * len(shape))

    def by_rows(n, width=columns):
        return pl.BlockSpec((n, width), lambda i, s: (i, 0))

    group_blocks = pl.BlockSpec((1, listed, group, group), lambda i, s: (i, 0, 0, 0))
    slab = whole(rows, columns)
    result = jax.ShapeDtypeStruct(c.shape, jnp.float32)
    half = jax.ShapeDtypeStruct(bblocks.shape, jnp.bfloat16)
    flops = 2 * rows * group * group * 3 * 3
    chunks = 2
    ring = [(i, (i + 1) % nb) for i in range(nb)]
    counter = [(j, i) for i, j in ring]
    even_pairs = [p for i in range(0, nb - 1, 2) for p in ((i, i + 1), (i + 1, i))]
    odd_pairs = [p for i in range(1, nb - 1, 2) for p in ((i, i + 1), (i + 1, i))]
    end_pairs = [(0, nb - 1), (nb - 1, 0)]

    def pick(chosen, c, *which):
        half_rows = rows // 2
        return pl.pallas_call(
            pick_kernel,
            grid_spec=pltpu.PrefetchScalarGridSpec(
                num_scalar_prefetch=1,
                grid=(2,),
                in_specs=[pl.BlockSpec((half_rows, group), lambda i, s, w=w: (i, s[w])) for w in which],
                out_specs=[by_rows(half_rows, group) for w in which],
            ),
            out_shape=[jax.ShapeDtypeStruct((rows, group), c.dtype) for w in which],
            name="pick",
        )(chosen, *[c for w in which])

    def own_groups(slots, c, ablocks, bblocks):
        return call(
            own_kernel, per,
            [slab, by_rows(group), group_blocks, whole(*bblocks.shape)],
            [by_rows(group), whole(*bblocks.shape), whole(*bblocks.shape)], [result, half, half],
            [(group, group)] * 4, 2 * flops, "own_groups", {},
        )(slots, c, c, ablocks, bblocks)

    def alpha_groups(slots, running, behind, ahead, ablocks):
        return call(
            alpha_kernel, per, [by_rows(group), slab, slab, group_blocks],
            by_rows(group), result, [(group, group)] * 4, 2 * flops, "alpha_groups", {1: 0},
        )(slots, running, behind, ahead, ablocks)

    def beta_groups(slots, running, high, low, arrived):
        def rows_of(x):
            return by_rows(rows // chunks, x.shape[1])

        return call(
            functools.partial(beta_kernel, [mask for mask, _ in arrived]), chunks,
            [rows_of(running)] + [rows_of(x) for _, x in arrived] + [whole(*bblocks.shape)] * 2,
            rows_of(running), result, [(rows // chunks, group)] * 2, flops, "beta_groups", {1: 0}, 20 * 1024 * 1024,
        )(slots, running, *[x for _, x in arrived], high, low)

    def branch(early, late):
        def body(c, near_odd, ablocks, bblocks, slots, chosen):
            which = [what for _, _, what in early + late if what in (to_ahead, to_behind, far_or_end)]
            picked = pick(chosen, c, *which) if which else []
            sources = {tile: c, near: near_odd, **dict(zip(which, picked, strict=True))}
            first = [(mask, lax.ppermute(sources[what], "beta", pairs)) for pairs, mask, what in early]
            a_behind = lax.ppermute(c, "alpha", [(i, (i + 1) % na) for i in range(na)])
            a_ahead = lax.ppermute(c, "alpha", [(i, (i - 1) % na) for i in range(na)])
            second = [(mask, lax.ppermute(sources[what], "beta", pairs)) for pairs, mask, what in late]
            running, high, low = own_groups(slots, c, ablocks, bblocks)
            running = beta_groups(slots, running, high, low, first)
            running = alpha_groups(slots, running, a_behind, a_ahead, ablocks)
            return beta_groups(slots, running, high, low, second)

        return body

    to_ahead, to_behind, far_or_end, near, tile = range(5)
    below, above = mask_of(sides=(BEHIND,)), mask_of(sides=(AHEAD,))
    even_kinds, odd_near = mask_of((EVEN,)), mask_of((ODD,), ranks=(NEAR,))
    far_or_end_kinds = mask_of((ODD,), ranks=(FAR,)) | mask_of((ENDS,))
    branches = [
        branch([(ring, below, to_ahead)], [(counter, above, to_behind)]),
        branch(
            [(odd_pairs, odd_near, near), (even_pairs, even_kinds, tile)],
            [(odd_pairs + end_pairs, far_or_end_kinds, far_or_end)],
        ),
        branch([(ring, below, tile)], [(counter, above, to_behind)]),
        branch([(counter, above, tile)], [(ring, below, to_ahead)]),
        branch([(ring, below, tile)], [(counter, above, tile)]),
    ]
    return lax.switch(index[0], branches, c, near_odd, ablocks, bblocks, slots, chosen)


def solution(mesh):
    in_specs = (
        P("alpha", "beta"),
        P("beta", None, None, None),
        P("alpha", None, None, None),
        P("beta", None),
        P("alpha", None),
        P("beta"),
        P("alpha"),
    )
    return jax.shard_map(
        on_device, mesh=mesh, in_specs=in_specs, out_specs=P("alpha", "beta"), check_vma=False
    )
```

```python
import functools

import jax
import jax.numpy as jnp
from jax import lax
from jax.experimental import pallas as pl
from jax.experimental.pallas import tpu as pltpu
from jax.sharding import PartitionSpec as P

VMEM_LIMIT = 56 * 1024 * 1024


def halves(x):
    high = x.astype(jnp.bfloat16)
    low = (x - high.astype(jnp.float32)).astype(jnp.bfloat16)
    return high, low


def split(x, high, low):
    high[...], low[...] = halves(x)


def add_product(out, left, right):
    (lh, ll), (rh, rl) = left, right
    dot = functools.partial(jnp.dot, preferred_element_type=jnp.float32)
    out[...] += dot(lh[...], rh[...]) + (dot(lh[...], rl[...]) + dot(ll[...], rh[...]))


def at(index, size):
    return pl.ds(pl.multiple_of(index * size, size), size)


OWN, UNUSED = 0, 13
EVEN, ODD, ENDS = range(3)
BEHIND, AHEAD = range(2)
NEAR, FAR = range(2)


def kind_of(pair, side, rank):
    return 1 + 4 * pair + 2 * side + rank


def mask_of(pairs=(EVEN, ODD, ENDS), sides=(BEHIND, AHEAD), ranks=(NEAR, FAR)):
    return sum(1 << kind_of(p, s, r) for p in pairs for s in sides for r in ranks)


def tables_kernel(owners, blinks, alinks, bcount, acount, slots, code):
    per, listed = blinks.shape
    (yn, zn), yi, zi = owners, lax.axis_index("alpha"), lax.axis_index("beta")
    first, last, even = zi == 0, zi == zn - 1, lax.rem(zi, 2) == 0
    pair_behind = jnp.where(first, ENDS, jnp.where(even, ODD, EVEN))
    pair_ahead = jnp.where(last, ENDS, jnp.where(even, EVEN, ODD))

    def where(links, count, g, l, index, n):
        slot = lax.rem(links[g, l] - index * per + per + n * per, n * per)
        return jnp.where(l < count[g], slot, -1)

    nb = fb = na = fa = jnp.int32(0)
    for g in range(per):
        for l in range(listed):
            slots[g * listed + l] = where(alinks, acount, g, l, yi, yn)
            slot = where(blinks, bcount, g, l, zi, zn)
            nb |= (slot == per - 1).astype(jnp.int32)
            fb |= (slot == per - 2).astype(jnp.int32)
            na |= (slot == 2 * per).astype(jnp.int32)
            fa |= (slot == 2 * per + 1).astype(jnp.int32)
            behind = kind_of(pair_behind, BEHIND, jnp.where(slot == per - 1, NEAR, FAR))
            ahead = kind_of(pair_ahead, AHEAD, jnp.where(slot == 2 * per, NEAR, FAR))
            kind = jnp.where(slot < per, behind, jnp.where(slot < 2 * per, OWN, ahead))
            kind = jnp.where(slot < 0, UNUSED, kind)
            slots[(per + g) * listed + l] = kind * per + lax.rem(slot + per, per)
    behind, ahead = nb + fb, na + fa
    climb = jnp.where(first, 0, behind >> 1)
    descend = jnp.where(last, 0, ahead >> 1)
    over = jnp.where(first, behind, 0)
    back = jnp.where(last, ahead, 0)
    code[0] = code[1] = climb + (descend << 6) + (over << 12) + (back << 14) + (nb << 16) + (na << 17)


def pick_kernel(chosen, *refs):
    for source, target in zip(refs[: len(refs) // 2], refs[len(refs) // 2 :], strict=True):
        target[...] = source[...]


def own_kernel(slots, tile, tile_rows, ablocks, bblocks, out, high, low, lh, ll, rh, rl):
    per, listed, group, _ = bblocks.shape
    row = pl.program_id(0)
    out[...] = jnp.zeros_like(out)

    def step(t, carry):
        g, l = t // listed, lax.rem(t, listed)
        a_slot, b_slot = slots[row * listed + l], slots[per * listed + t]

        @pl.when(row == 0)
        def _():
            split(bblocks[g, l], high.at[g, l], low.at[g, l])

        @pl.when((a_slot >= per) & (a_slot < 2 * per))
        def _():
            split(ablocks[0, l], lh, ll)
            split(tile[at(a_slot - per, group), at(g, group)], rh, rl)
            add_product(out.at[:, at(g, group)], (lh, ll), (rh, rl))

        @pl.when(lax.div(b_slot, per) == OWN)
        def _():
            split(tile_rows[:, at(b_slot, group)], lh, ll)
            add_product(out.at[:, at(g, group)], (lh, ll), (high.at[g, l], low.at[g, l]))

        return carry

    lax.fori_loop(0, per * listed, step, 0)


def alpha_kernel(slots, running, behind, ahead, ablocks, out, lh, ll, rh, rl):
    _, listed, group, _ = ablocks.shape
    per = behind.shape[0] // group
    row = pl.program_id(0)
    out[...] = running[...]

    def step(t, carry):
        l, g = t // per, lax.rem(t, per)
        slot = slots[row * listed + l]
        below, above = (slot >= 0) & (slot < per), slot >= 2 * per
        for inside, tile, base in ((below, behind, 0), (above, ahead, 2 * per)):

            @pl.when(inside)
            def _(tile=tile, base=base):
                split(tile[at(slot - base, group), at(g, group)], rh, rl)

        @pl.when((below | above) & (g == 0))
        def _():
            split(ablocks[0, l], lh, ll)

        @pl.when(below | above)
        def _():
            add_product(out.at[:, at(g, group)], (lh, ll), (rh, rl))

        return carry

    lax.fori_loop(0, per * listed, step, 0)


def beta_kernel(masks, slots, running, *refs):
    *buffers, high, low, out, lh, ll = refs
    per, listed, group, _ = high.shape
    out[...] = running[...]

    def step(t, carry):
        g, l = t // listed, lax.rem(t, listed)
        slot = slots[per * listed + t]
        hits = []
        for mask, tile in zip(masks, buffers, strict=True):
            hits.append(((mask >> lax.div(slot, per)) & 1) == 1)

            @pl.when(hits[-1])
            def _(tile=tile):
                part = tile[...] if tile.shape[1] == group else tile[:, at(lax.rem(slot, per), group)]
                split(part, lh, ll)

        @pl.when(functools.reduce(jnp.logical_or, hits))
        def _():
            add_product(out.at[:, at(g, group)], (lh, ll), (high.at[g, l], low.at[g, l]))

        return carry

    lax.fori_loop(0, per * listed, step, 0)


def call(kernel, grid, in_specs, out_spec, shape, scratch, flops, name, aliases, vmem=VMEM_LIMIT):
    return pl.pallas_call(
        kernel,
        grid_spec=pltpu.PrefetchScalarGridSpec(
            num_scalar_prefetch=1, grid=(grid,), in_specs=in_specs, out_specs=out_spec,
            scratch_shapes=[pltpu.VMEM(x, jnp.bfloat16) for x in scratch],
        ),
        out_shape=shape,
        input_output_aliases=aliases,
        compiler_params=pltpu.CompilerParams(vmem_limit_bytes=vmem),
        cost_estimate=pl.CostEstimate(flops=flops, bytes_accessed=16 * 1024 * 1024, transcendentals=0),
        name=name,
    )


def on_device(c, bblocks, ablocks, blinks, alinks, bcount, acount):
    rows, columns = c.shape
    per, listed, group, _ = ablocks.shape
    na, nb = lax.axis_size("alpha"), lax.axis_size("beta")
    smem = pl.BlockSpec(memory_space=pltpu.SMEM)
    slots, code = pl.pallas_call(
        functools.partial(tables_kernel, (na, nb)),
        in_specs=[smem] * 4,
        out_specs=[smem] * 2,
        out_shape=[jax.ShapeDtypeStruct((2 * per * listed,), jnp.int32), jax.ShapeDtypeStruct((2,), jnp.int32)],
        name="tables",
    )(blinks, alinks, bcount, acount)

    codes = [code] + [
        lax.ppermute(code, "beta", [(i, (i + by) % nb) for i in range(nb)]) for by in range(1, nb)
    ]
    z = lax.axis_index("beta")
    even = z % 2 == 0
    near_odd = lax.dynamic_slice_in_dim(c, jnp.where(even, 0, per - 1) * group, group, 1)
    *codes, near_odd = lax.optimization_barrier((*codes, near_odd))
    total = functools.reduce(lambda x, y: x + y, [x & 0xFFFF for x in codes])
    climb, descend = (total & 0x3F) > 0, (total & 0xFC0) > 0
    over, back = (total & 0x3000) == 0x2000, (total & 0xC000) == 0x8000
    full = (climb & back) | (descend & over) | (over & back)
    some = (climb | descend).astype(jnp.int32)
    index = jnp.where(full, 4, jnp.where(over, 2, jnp.where(back, 3, some)))
    to_ahead = jnp.where((codes[nb - 1] & 0x10000) > 0, per - 1, per - 2)
    to_behind = jnp.where((codes[1] & 0x20000) > 0, 0, 1)
    far_odd = jnp.where(even, 1, per - 2)
    to_end = jnp.where(even, to_behind, to_ahead)
    chosen = jnp.stack([to_ahead, to_behind, jnp.where((z == 0) | (z == nb - 1), to_end, far_odd)])[:, 0]

    def whole(*shape):
        return pl.BlockSpec(shape, lambda i, s: (0,) * len(shape))

    def by_rows(n, width=columns):
        return pl.BlockSpec((n, width), lambda i, s: (i, 0))

    group_blocks = pl.BlockSpec((1, listed, group, group), lambda i, s: (i, 0, 0, 0))
    slab = whole(rows, columns)
    result = jax.ShapeDtypeStruct(c.shape, jnp.float32)
    half = jax.ShapeDtypeStruct(bblocks.shape, jnp.bfloat16)
    flops = 2 * rows * group * group * 3 * 3
    ring = [(i, (i + 1) % nb) for i in range(nb)]
    counter = [(j, i) for i, j in ring]
    even_pairs = [p for i in range(0, nb - 1, 2) for p in ((i, i + 1), (i + 1, i))]
    odd_pairs = [p for i in range(1, nb - 1, 2) for p in ((i, i + 1), (i + 1, i))]
    end_pairs = [(0, nb - 1), (nb - 1, 0)]

    def pick(chosen, c, pieces):
        def source(what, r, n):
            return pl.BlockSpec((rows // n, group), lambda i, s: (r, s[what]))

        return pl.pallas_call(
            pick_kernel,
            grid_spec=pltpu.PrefetchScalarGridSpec(
                num_scalar_prefetch=1,
                grid=(1,),
                in_specs=[source(*piece) for piece in pieces],
                out_specs=[whole(rows // n, group) for _, _, n in pieces],
            ),
            out_shape=[jax.ShapeDtypeStruct((rows // n, group), c.dtype) for _, _, n in pieces],
            name="pick",
        )(chosen, *[c for _ in pieces])

    def own_groups(slots, c, ablocks, bblocks):
        return call(
            own_kernel, per,
            [slab, by_rows(group), group_blocks, whole(*bblocks.shape)],
            [by_rows(group), whole(*bblocks.shape), whole(*bblocks.shape)], [result, half, half],
            [(group, group)] * 4, 2 * flops, "own_groups", {},
        )(slots, c, c, ablocks, bblocks)

    def alpha_groups(slots, running, behind, ahead, ablocks):
        return call(
            alpha_kernel, per, [by_rows(group), slab, slab, group_blocks],
            by_rows(group), result, [(group, group)] * 4, 2 * flops, "alpha_groups", {1: 0},
        )(slots, running, behind, ahead, ablocks)

    def beta_groups(slots, running, high, low, arrived, r=None):
        mask, buffer = arrived
        height = rows // 2
        of_running = pl.BlockSpec((height, columns), lambda i, s: (i if r is None else r, 0))
        return call(
            functools.partial(beta_kernel, [mask]), 2 if r is None else 1,
            [of_running, by_rows(height, buffer.shape[1])] + [whole(*bblocks.shape)] * 2,
            of_running, result, [(height, group)] * 2, flops, "beta_groups", {1: 0}, 20 * 1024 * 1024,
        )(slots, running, buffer, high, low)

    def branch(early, late):
        def body(c, near_odd, ablocks, bblocks, slots, chosen):
            sends = [(*send, 0, 1) for send in early] + [(*late, r, 2) for r in range(2)]
            pieces = [(what, r, n) for _, _, what, r, n in sends if what not in (tile, near)]
            picked = dict(zip(pieces, pick(chosen, c, pieces), strict=True)) if pieces else {}

            def start(pairs, mask, what, r, n):
                if what == tile:
                    x = c[r * (rows // n) : (r + 1) * (rows // n)]
                else:
                    x = near_odd if what == near else picked[what, r, n]
                return mask, lax.ppermute(x, "beta", pairs)

            arrivals = [start(*send) for send in sends]
            a_behind = lax.ppermute(c, "alpha", [(i, (i + 1) % na) for i in range(na)])
            a_ahead = lax.ppermute(c, "alpha", [(i, (i - 1) % na) for i in range(na)])
            running, high, low = own_groups(slots, c, ablocks, bblocks)
            for arrived in arrivals[:-2]:
                running = beta_groups(slots, running, high, low, arrived)
            running = alpha_groups(slots, running, a_behind, a_ahead, ablocks)
            for r, arrived in enumerate(arrivals[-2:]):
                running = beta_groups(slots, running, high, low, arrived, r)
            return running

        return body

    to_ahead, to_behind, far_or_end, near, tile = range(5)
    below, above = mask_of(sides=(BEHIND,)), mask_of(sides=(AHEAD,))
    even_kinds, odd_near = mask_of((EVEN,)), mask_of((ODD,), ranks=(NEAR,))
    far_or_end_kinds = mask_of((ODD,), ranks=(FAR,)) | mask_of((ENDS,))
    branches = [
        branch([(ring, below, to_ahead)], (counter, above, to_behind)),
        branch(
            [(odd_pairs, odd_near, near), (even_pairs, even_kinds, tile)],
            (odd_pairs + end_pairs, far_or_end_kinds, far_or_end),
        ),
        branch([(ring, below, tile)], (counter, above, to_behind)),
        branch([(counter, above, tile)], (ring, below, to_ahead)),
        branch([(ring, below, tile)], (counter, above, tile)),
    ]
    return lax.switch(index[0], branches, c, near_odd, ablocks, bblocks, slots, chosen)


def solution(mesh):
    in_specs = (
        P("alpha", "beta"),
        P("beta", None, None, None),
        P("alpha", None, None, None),
        P("beta", None),
        P("alpha", None),
        P("beta"),
        P("alpha"),
    )
    return jax.shard_map(
        on_device, mesh=mesh, in_specs=in_specs, out_specs=P("alpha", "beta"), check_vma=False
    )
```

```python
import functools

import jax
import jax.numpy as jnp
from jax import lax
from jax.experimental import pallas as pl
from jax.experimental.pallas import tpu as pltpu
from jax.sharding import PartitionSpec as P

VMEM_LIMIT = 56 * 1024 * 1024


def halves(x):
    high = x.astype(jnp.bfloat16)
    low = (x - high.astype(jnp.float32)).astype(jnp.bfloat16)
    return high, low


def split(x, high, low):
    high[...], low[...] = halves(x)


def add_product(out, left, right):
    (lh, ll), (rh, rl) = left, right
    dot = functools.partial(jnp.dot, preferred_element_type=jnp.float32)
    out[...] += dot(lh[...], rh[...]) + (dot(lh[...], rl[...]) + dot(ll[...], rh[...]))


def at(index, size):
    return pl.ds(pl.multiple_of(index * size, size), size)


OWN, UNUSED = 0, 13
EVEN, ODD, ENDS = range(3)
BEHIND, AHEAD = range(2)
NEAR, FAR = range(2)


def kind_of(pair, side, rank):
    return 1 + 4 * pair + 2 * side + rank


def mask_of(pairs=(EVEN, ODD, ENDS), sides=(BEHIND, AHEAD), ranks=(NEAR, FAR)):
    return sum(1 << kind_of(p, s, r) for p in pairs for s in sides for r in ranks)


def tables_kernel(owners, blinks, alinks, bcount, acount, slots, code):
    per, listed = blinks.shape
    (yn, zn), yi, zi = owners, lax.axis_index("alpha"), lax.axis_index("beta")
    first, last, even = zi == 0, zi == zn - 1, lax.rem(zi, 2) == 0
    pair_behind = jnp.where(first, ENDS, jnp.where(even, ODD, EVEN))
    pair_ahead = jnp.where(last, ENDS, jnp.where(even, EVEN, ODD))

    def where(links, count, g, l, index, n):
        slot = lax.rem(links[g, l] - index * per + per + n * per, n * per)
        return jnp.where(l < count[g], slot, -1)

    nb = fb = na = fa = jnp.int32(0)
    for g in range(per):
        for l in range(listed):
            slots[g * listed + l] = where(alinks, acount, g, l, yi, yn)
            slot = where(blinks, bcount, g, l, zi, zn)
            nb |= (slot == per - 1).astype(jnp.int32)
            fb |= (slot == per - 2).astype(jnp.int32)
            na |= (slot == 2 * per).astype(jnp.int32)
            fa |= (slot == 2 * per + 1).astype(jnp.int32)
            behind = kind_of(pair_behind, BEHIND, jnp.where(slot == per - 1, NEAR, FAR))
            ahead = kind_of(pair_ahead, AHEAD, jnp.where(slot == 2 * per, NEAR, FAR))
            kind = jnp.where(slot < per, behind, jnp.where(slot < 2 * per, OWN, ahead))
            kind = jnp.where(slot < 0, UNUSED, kind)
            slots[(per + g) * listed + l] = kind * per + lax.rem(slot + per, per)
    behind, ahead = nb + fb, na + fa
    climb = jnp.where(first, 0, behind >> 1)
    descend = jnp.where(last, 0, ahead >> 1)
    over = jnp.where(first, behind, 0)
    back = jnp.where(last, ahead, 0)
    code[0] = code[1] = climb + (descend << 6) + (over << 12) + (back << 14) + (nb << 16) + (na << 17)


def pick_kernel(chosen, *refs):
    for source, target in zip(refs[: len(refs) // 2], refs[len(refs) // 2 :], strict=True):
        target[...] = source[...]


def own_kernel(slots, tile, tile_rows, ablocks, bblocks, out, high, low, lh, ll, rh, rl):
    per, listed, group, _ = bblocks.shape
    row = pl.program_id(0)
    out[...] = jnp.zeros_like(out)

    def step(t, carry):
        g, l = t // listed, lax.rem(t, listed)
        a_slot, b_slot = slots[row * listed + l], slots[per * listed + t]

        @pl.when(row == 0)
        def _():
            split(bblocks[g, l], high.at[g, l], low.at[g, l])

        @pl.when((a_slot >= per) & (a_slot < 2 * per))
        def _():
            split(ablocks[0, l], lh, ll)
            split(tile[at(a_slot - per, group), at(g, group)], rh, rl)
            add_product(out.at[:, at(g, group)], (lh, ll), (rh, rl))

        @pl.when(lax.div(b_slot, per) == OWN)
        def _():
            split(tile_rows[:, at(b_slot, group)], lh, ll)
            add_product(out.at[:, at(g, group)], (lh, ll), (high.at[g, l], low.at[g, l]))

        return carry

    lax.fori_loop(0, per * listed, step, 0)


def alpha_kernel(slots, running, behind, ahead, ablocks, out, lh, ll, rh, rl):
    _, listed, group, _ = ablocks.shape
    per = behind.shape[0] // group
    row = pl.program_id(0)
    out[...] = running[...]

    def step(t, carry):
        l, g = t // per, lax.rem(t, per)
        slot = slots[row * listed + l]
        below, above = (slot >= 0) & (slot < per), slot >= 2 * per
        for inside, tile, base in ((below, behind, 0), (above, ahead, 2 * per)):

            @pl.when(inside)
            def _(tile=tile, base=base):
                split(tile[at(slot - base, group), at(g, group)], rh, rl)

        @pl.when((below | above) & (g == 0))
        def _():
            split(ablocks[0, l], lh, ll)

        @pl.when(below | above)
        def _():
            add_product(out.at[:, at(g, group)], (lh, ll), (rh, rl))

        return carry

    lax.fori_loop(0, per * listed, step, 0)


def beta_kernel(masks, slots, running, *refs):
    *buffers, high, low, out, lh, ll = refs
    per, listed, group, _ = high.shape
    out[...] = running[...]

    def step(t, carry):
        g, l = t // listed, lax.rem(t, listed)
        slot = slots[per * listed + t]
        hits = []
        for mask, tile in zip(masks, buffers, strict=True):
            hits.append(((mask >> lax.div(slot, per)) & 1) == 1)

            @pl.when(hits[-1])
            def _(tile=tile):
                part = tile[...] if tile.shape[1] == group else tile[:, at(lax.rem(slot, per), group)]
                split(part, lh, ll)

        @pl.when(functools.reduce(jnp.logical_or, hits))
        def _():
            add_product(out.at[:, at(g, group)], (lh, ll), (high.at[g, l], low.at[g, l]))

        return carry

    lax.fori_loop(0, per * listed, step, 0)


def call(kernel, grid, in_specs, out_spec, shape, scratch, flops, name, aliases, vmem=VMEM_LIMIT):
    return pl.pallas_call(
        kernel,
        grid_spec=pltpu.PrefetchScalarGridSpec(
            num_scalar_prefetch=1, grid=(grid,), in_specs=in_specs, out_specs=out_spec,
            scratch_shapes=[pltpu.VMEM(x, jnp.bfloat16) for x in scratch],
        ),
        out_shape=shape,
        input_output_aliases=aliases,
        compiler_params=pltpu.CompilerParams(vmem_limit_bytes=vmem),
        cost_estimate=pl.CostEstimate(flops=flops, bytes_accessed=16 * 1024 * 1024, transcendentals=0),
        name=name,
    )


def on_device(c, bblocks, ablocks, blinks, alinks, bcount, acount):
    rows, columns = c.shape
    per, listed, group, _ = ablocks.shape
    na, nb = lax.axis_size("alpha"), lax.axis_size("beta")
    smem = pl.BlockSpec(memory_space=pltpu.SMEM)
    slots, code = pl.pallas_call(
        functools.partial(tables_kernel, (na, nb)),
        in_specs=[smem] * 4,
        out_specs=[smem] * 2,
        out_shape=[jax.ShapeDtypeStruct((2 * per * listed,), jnp.int32), jax.ShapeDtypeStruct((2,), jnp.int32)],
        name="tables",
    )(blinks, alinks, bcount, acount)

    codes = [code] + [
        lax.ppermute(code, "beta", [(i, (i + by) % nb) for i in range(nb)]) for by in range(1, nb)
    ]
    z = lax.axis_index("beta")
    even = z % 2 == 0
    near_odd = lax.dynamic_slice_in_dim(c, jnp.where(even, 0, per - 1) * group, group, 1)
    *codes, near_odd = lax.optimization_barrier((*codes, near_odd))
    total = functools.reduce(lambda x, y: x + y, [x & 0xFFFF for x in codes])
    climb, descend = (total & 0x3F) > 0, (total & 0xFC0) > 0
    over, back = (total & 0x3000) == 0x2000, (total & 0xC000) == 0x8000
    full = (climb & back) | (descend & over) | (over & back)
    some = (climb | descend).astype(jnp.int32)
    index = jnp.where(full, 4, jnp.where(over, 2, jnp.where(back, 3, some)))
    to_ahead = jnp.where((codes[nb - 1] & 0x10000) > 0, per - 1, per - 2)
    to_behind = jnp.where((codes[1] & 0x20000) > 0, 0, 1)
    far_odd = jnp.where(even, 1, per - 2)
    to_end = jnp.where(even, to_behind, to_ahead)
    chosen = jnp.stack([to_ahead, to_behind, jnp.where((z == 0) | (z == nb - 1), to_end, far_odd)])[:, 0]

    def whole(*shape):
        return pl.BlockSpec(shape, lambda i, s: (0,) * len(shape))

    def by_rows(n, width=columns):
        return pl.BlockSpec((n, width), lambda i, s: (i, 0))

    group_blocks = pl.BlockSpec((1, listed, group, group), lambda i, s: (i, 0, 0, 0))
    slab = whole(rows, columns)
    result = jax.ShapeDtypeStruct(c.shape, jnp.float32)
    half = jax.ShapeDtypeStruct(bblocks.shape, jnp.bfloat16)
    flops = 2 * rows * group * group * 3 * 3
    ring = [(i, (i + 1) % nb) for i in range(nb)]
    counter = [(j, i) for i, j in ring]
    even_pairs = [p for i in range(0, nb - 1, 2) for p in ((i, i + 1), (i + 1, i))]
    odd_pairs = [p for i in range(1, nb - 1, 2) for p in ((i, i + 1), (i + 1, i))]
    end_pairs = [(0, nb - 1), (nb - 1, 0)]

    quarter = rows // 4
    whole_rows, most_rows, last_rows = (0, 4), (0, 3), (3, 4)

    def pick(chosen, c, pieces):
        def source(what, part):
            height = (part[1] - part[0]) * quarter
            return pl.BlockSpec((height, group), lambda i, s: (part[0] * quarter // height, s[what]))

        heights = [(part[1] - part[0]) * quarter for _, part in pieces]
        return pl.pallas_call(
            pick_kernel,
            grid_spec=pltpu.PrefetchScalarGridSpec(
                num_scalar_prefetch=1,
                grid=(1,),
                in_specs=[source(*piece) for piece in pieces],
                out_specs=[whole(height, group) for height in heights],
            ),
            out_shape=[jax.ShapeDtypeStruct((height, group), c.dtype) for height in heights],
            name="pick",
        )(chosen, *[c for _ in pieces])

    def own_groups(slots, c, ablocks, bblocks):
        return call(
            own_kernel, per,
            [slab, by_rows(group), group_blocks, whole(*bblocks.shape)],
            [by_rows(group), whole(*bblocks.shape), whole(*bblocks.shape)], [result, half, half],
            [(group, group)] * 4, 2 * flops, "own_groups", {},
        )(slots, c, c, ablocks, bblocks)

    def alpha_groups(slots, running, behind, ahead, ablocks):
        return call(
            alpha_kernel, per, [by_rows(group), slab, slab, group_blocks],
            by_rows(group), result, [(group, group)] * 4, 2 * flops, "alpha_groups", {1: 0},
        )(slots, running, behind, ahead, ablocks)

    def beta_groups(slots, running, high, low, arrived):
        mask, part, buffer = arrived
        of_running = pl.BlockSpec((quarter, columns), lambda i, s: (part[0] + i, 0))
        return call(
            functools.partial(beta_kernel, [mask]), part[1] - part[0],
            [of_running, by_rows(quarter, buffer.shape[1])] + [whole(*bblocks.shape)] * 2,
            of_running, result, [(quarter, group)] * 2, flops, "beta_groups", {1: 0}, 20 * 1024 * 1024,
        )(slots, running, buffer, high, low)

    def branch(early, late):
        def body(c, near_odd, ablocks, bblocks, slots, chosen):
            sends = [(*send, whole_rows) for send in early] + [(*late, part) for part in (most_rows, last_rows)]
            pieces = [(what, part) for _, _, what, part in sends if what not in (tile, near)]
            picked = dict(zip(pieces, pick(chosen, c, pieces), strict=True)) if pieces else {}

            def start(pairs, mask, what, part):
                if what == tile:
                    x = c[part[0] * quarter : part[1] * quarter]
                else:
                    x = near_odd if what == near else picked[what, part]
                return mask, part, lax.ppermute(x, "beta", pairs)

            arrivals = [start(*send) for send in sends]
            a_behind = lax.ppermute(c, "alpha", [(i, (i + 1) % na) for i in range(na)])
            a_ahead = lax.ppermute(c, "alpha", [(i, (i - 1) % na) for i in range(na)])
            running, high, low = own_groups(slots, c, ablocks, bblocks)
            for arrived in arrivals[:-2]:
                running = beta_groups(slots, running, high, low, arrived)
            running = alpha_groups(slots, running, a_behind, a_ahead, ablocks)
            for arrived in arrivals[-2:]:
                running = beta_groups(slots, running, high, low, arrived)
            return running

        return body

    to_ahead, to_behind, far_or_end, near, tile = range(5)
    below, above = mask_of(sides=(BEHIND,)), mask_of(sides=(AHEAD,))
    even_kinds, odd_near = mask_of((EVEN,)), mask_of((ODD,), ranks=(NEAR,))
    far_or_end_kinds = mask_of((ODD,), ranks=(FAR,)) | mask_of((ENDS,))
    branches = [
        branch([(ring, below, to_ahead)], (counter, above, to_behind)),
        branch(
            [(odd_pairs, odd_near, near), (even_pairs, even_kinds, tile)],
            (odd_pairs + end_pairs, far_or_end_kinds, far_or_end),
        ),
        branch([(ring, below, tile)], (counter, above, to_behind)),
        branch([(counter, above, tile)], (ring, below, to_ahead)),
        branch([(ring, below, tile)], (counter, above, tile)),
    ]
    return lax.switch(index[0], branches, c, near_odd, ablocks, bblocks, slots, chosen)


def solution(mesh):
    in_specs = (
        P("alpha", "beta"),
        P("beta", None, None, None),
        P("alpha", None, None, None),
        P("beta", None),
        P("alpha", None),
        P("beta"),
        P("alpha"),
    )
    return jax.shard_map(
        on_device, mesh=mesh, in_specs=in_specs, out_specs=P("alpha", "beta"), check_vma=False
    )
```

```python
import functools

import jax
import jax.numpy as jnp
from jax import lax
from jax.experimental import pallas as pl
from jax.experimental.pallas import tpu as pltpu
from jax.sharding import PartitionSpec as P

VMEM_LIMIT = 56 * 1024 * 1024


def halves(x):
    high = x.astype(jnp.bfloat16)
    low = (x - high.astype(jnp.float32)).astype(jnp.bfloat16)
    return high, low


def split(x, high, low):
    height = 192

    def step(i, carry):
        rows = at(i, height)
        high[rows, :], low[rows, :] = halves(x[rows, :])
        return carry

    lax.fori_loop(0, high.shape[0] // height, step, 0)


def add_product(out, left, right, height):
    (lh, ll), (rh, rl) = left, right
    dot = functools.partial(jnp.dot, preferred_element_type=jnp.float32)

    def step(i, carry):
        rows = at(i, height)
        high, low = lh[rows, :], ll[rows, :]
        out[rows, :] += dot(high, rh[...]) + (dot(high, rl[...]) + dot(low, rh[...]))
        return carry

    lax.fori_loop(0, lh.shape[0] // height, step, 0)


def at(index, size):
    return pl.ds(pl.multiple_of(index * size, size), size)


OWN, UNUSED = 0, 13
EVEN, ODD, ENDS = range(3)
BEHIND, AHEAD = range(2)
NEAR, FAR = range(2)


def kind_of(pair, side, rank):
    return 1 + 4 * pair + 2 * side + rank


def mask_of(pairs=(EVEN, ODD, ENDS), sides=(BEHIND, AHEAD), ranks=(NEAR, FAR)):
    return sum(1 << kind_of(p, s, r) for p in pairs for s in sides for r in ranks)


def tables_kernel(owners, blinks, alinks, bcount, acount, slots, code):
    per, listed = blinks.shape
    (yn, zn), yi, zi = owners, lax.axis_index("alpha"), lax.axis_index("beta")
    first, last, even = zi == 0, zi == zn - 1, lax.rem(zi, 2) == 0
    pair_behind = jnp.where(first, ENDS, jnp.where(even, ODD, EVEN))
    pair_ahead = jnp.where(last, ENDS, jnp.where(even, EVEN, ODD))

    def where(links, count, g, l, index, n):
        slot = lax.rem(links[g, l] - index * per + per + n * per, n * per)
        return jnp.where(l < count[g], slot, -1)

    nb = fb = na = fa = jnp.int32(0)
    for g in range(per):
        for l in range(listed):
            slots[g * listed + l] = where(alinks, acount, g, l, yi, yn)
            slot = where(blinks, bcount, g, l, zi, zn)
            nb |= (slot == per - 1).astype(jnp.int32)
            fb |= (slot == per - 2).astype(jnp.int32)
            na |= (slot == 2 * per).astype(jnp.int32)
            fa |= (slot == 2 * per + 1).astype(jnp.int32)
            behind = kind_of(pair_behind, BEHIND, jnp.where(slot == per - 1, NEAR, FAR))
            ahead = kind_of(pair_ahead, AHEAD, jnp.where(slot == 2 * per, NEAR, FAR))
            kind = jnp.where(slot < per, behind, jnp.where(slot < 2 * per, OWN, ahead))
            kind = jnp.where(slot < 0, UNUSED, kind)
            slots[(per + g) * listed + l] = kind * per + lax.rem(slot + per, per)
    behind, ahead = nb + fb, na + fa
    climb = jnp.where(first, 0, behind >> 1)
    descend = jnp.where(last, 0, ahead >> 1)
    over = jnp.where(first, behind, 0)
    back = jnp.where(last, ahead, 0)
    code[0] = code[1] = climb + (descend << 6) + (over << 12) + (back << 14) + (nb << 16) + (na << 17)


def pick_kernel(chosen, *refs):
    for source, target in zip(refs[: len(refs) // 2], refs[len(refs) // 2 :], strict=True):
        target[...] = source[...]


def own_kernel(slots, tile, tile_rows, ablocks, bblocks, out, high, low, lh, ll, rh, rl):
    per, listed, group, _ = bblocks.shape
    row = pl.program_id(0)
    out[...] = jnp.zeros_like(out)

    def step(t, carry):
        g, l = t // listed, lax.rem(t, listed)
        a_slot, b_slot = slots[row * listed + l], slots[per * listed + t]

        @pl.when(row == 0)
        def _():
            split(bblocks.at[g, l], high.at[g, l], low.at[g, l])

        @pl.when((a_slot >= per) & (a_slot < 2 * per))
        def _():
            split(ablocks.at[0, l], lh, ll)
            split(tile.at[at(a_slot - per, group), at(g, group)], rh, rl)
            add_product(out.at[:, at(g, group)], (lh, ll), (rh, rl), 192)

        @pl.when(lax.div(b_slot, per) == OWN)
        def _():
            split(tile_rows.at[:, at(b_slot, group)], lh, ll)
            add_product(out.at[:, at(g, group)], (lh, ll), (high.at[g, l], low.at[g, l]), 192)

        return carry

    lax.fori_loop(0, per * listed, step, 0)


def alpha_kernel(slots, running, behind, ahead, ablocks, out, lh, ll, rh, rl):
    _, listed, group, _ = ablocks.shape
    per = behind.shape[0] // group
    row = pl.program_id(0)
    out[...] = running[...]

    def step(t, carry):
        l, g = t // per, lax.rem(t, per)
        slot = slots[row * listed + l]
        below, above = (slot >= 0) & (slot < per), slot >= 2 * per
        for inside, tile, base in ((below, behind, 0), (above, ahead, 2 * per)):

            @pl.when(inside)
            def _(tile=tile, base=base):
                split(tile.at[at(slot - base, group), at(g, group)], rh, rl)

        @pl.when((below | above) & (g == 0))
        def _():
            split(ablocks.at[0, l], lh, ll)

        @pl.when(below | above)
        def _():
            add_product(out.at[:, at(g, group)], (lh, ll), (rh, rl), 192)

        return carry

    lax.fori_loop(0, per * listed, step, 0)


def beta_kernel(masks, slots, running, *refs):
    *buffers, high, low, out, lh, ll = refs
    per, listed, group, _ = high.shape
    out[...] = running[...]

    def step(t, carry):
        g, l = t // listed, lax.rem(t, listed)
        slot = slots[per * listed + t]
        hits = []
        for mask, tile in zip(masks, buffers, strict=True):
            hits.append(((mask >> lax.div(slot, per)) & 1) == 1)

            @pl.when(hits[-1])
            def _(tile=tile):
                part = tile if tile.shape[1] == group else tile.at[:, at(lax.rem(slot, per), group)]
                split(part, lh, ll)

        @pl.when(functools.reduce(jnp.logical_or, hits))
        def _():
            add_product(out.at[:, at(g, group)], (lh, ll), (high.at[g, l], low.at[g, l]), 192)

        return carry

    lax.fori_loop(0, per * listed, step, 0)


def call(kernel, grid, in_specs, out_spec, shape, scratch, flops, name, aliases, vmem=VMEM_LIMIT):
    return pl.pallas_call(
        kernel,
        grid_spec=pltpu.PrefetchScalarGridSpec(
            num_scalar_prefetch=1, grid=(grid,), in_specs=in_specs, out_specs=out_spec,
            scratch_shapes=[pltpu.VMEM(x, jnp.bfloat16) for x in scratch],
        ),
        out_shape=shape,
        input_output_aliases=aliases,
        compiler_params=pltpu.CompilerParams(vmem_limit_bytes=vmem),
        cost_estimate=pl.CostEstimate(flops=flops, bytes_accessed=16 * 1024 * 1024, transcendentals=0),
        name=name,
    )


def on_device(c, bblocks, ablocks, blinks, alinks, bcount, acount):
    rows, columns = c.shape
    per, listed, group, _ = ablocks.shape
    na, nb = lax.axis_size("alpha"), lax.axis_size("beta")
    smem = pl.BlockSpec(memory_space=pltpu.SMEM)
    slots, code = pl.pallas_call(
        functools.partial(tables_kernel, (na, nb)),
        in_specs=[smem] * 4,
        out_specs=[smem] * 2,
        out_shape=[jax.ShapeDtypeStruct((2 * per * listed,), jnp.int32), jax.ShapeDtypeStruct((2,), jnp.int32)],
        name="tables",
    )(blinks, alinks, bcount, acount)

    codes = [code] + [
        lax.ppermute(code, "beta", [(i, (i + by) % nb) for i in range(nb)]) for by in range(1, nb)
    ]
    z = lax.axis_index("beta")
    even = z % 2 == 0
    near_odd = lax.dynamic_slice_in_dim(c, jnp.where(even, 0, per - 1) * group, group, 1)
    *codes, near_odd = lax.optimization_barrier((*codes, near_odd))
    total = functools.reduce(lambda x, y: x + y, [x & 0xFFFF for x in codes])
    climb, descend = (total & 0x3F) > 0, (total & 0xFC0) > 0
    over, back = (total & 0x3000) == 0x2000, (total & 0xC000) == 0x8000
    full = (climb & back) | (descend & over) | (over & back)
    index = jnp.where(full, 1, jnp.where(over, 2, jnp.where(back, 3, jnp.where(climb | descend, 0, 4))))
    to_ahead = jnp.where((codes[nb - 1] & 0x10000) > 0, per - 1, per - 2)
    to_behind = jnp.where((codes[1] & 0x20000) > 0, 0, 1)
    far_odd = jnp.where(even, 1, per - 2)
    to_end = jnp.where(even, to_behind, to_ahead)
    chosen = jnp.stack([to_ahead, to_behind, jnp.where((z == 0) | (z == nb - 1), to_end, far_odd)])[:, 0]

    def whole(*shape):
        return pl.BlockSpec(shape, lambda i, s: (0,) * len(shape))

    def by_rows(n, width=columns):
        return pl.BlockSpec((n, width), lambda i, s: (i, 0))

    group_blocks = pl.BlockSpec((1, listed, group, group), lambda i, s: (i, 0, 0, 0))
    slab = whole(rows, columns)
    result = jax.ShapeDtypeStruct(c.shape, jnp.float32)
    half = jax.ShapeDtypeStruct(bblocks.shape, jnp.bfloat16)
    flops = 2 * rows * group * group * 3 * 3
    ring = [(i, (i + 1) % nb) for i in range(nb)]
    counter = [(j, i) for i, j in ring]
    even_pairs = [p for i in range(0, nb - 1, 2) for p in ((i, i + 1), (i + 1, i))]
    odd_pairs = [p for i in range(1, nb - 1, 2) for p in ((i, i + 1), (i + 1, i))]
    end_pairs = [(0, nb - 1), (nb - 1, 0)]

    quarter = rows // 4
    whole_rows, most_rows, last_rows = (0, 4), (0, 3), (3, 4)

    def pick(chosen, c, pieces):
        def source(what, part):
            height = (part[1] - part[0]) * quarter
            return pl.BlockSpec((height, group), lambda i, s: (part[0] * quarter // height, s[what]))

        heights = [(part[1] - part[0]) * quarter for _, part in pieces]
        return pl.pallas_call(
            pick_kernel,
            grid_spec=pltpu.PrefetchScalarGridSpec(
                num_scalar_prefetch=1,
                grid=(1,),
                in_specs=[source(*piece) for piece in pieces],
                out_specs=[whole(height, group) for height in heights],
            ),
            out_shape=[jax.ShapeDtypeStruct((height, group), c.dtype) for height in heights],
            name="pick",
        )(chosen, *[c for _ in pieces])

    def own_groups(slots, c, ablocks, bblocks):
        return call(
            own_kernel, per,
            [slab, by_rows(group), group_blocks, whole(*bblocks.shape)],
            [by_rows(group), whole(*bblocks.shape), whole(*bblocks.shape)], [result, half, half],
            [(group, group)] * 4, 2 * flops, "own_groups", {},
        )(slots, c, c, ablocks, bblocks)

    def alpha_groups(slots, running, behind, ahead, ablocks):
        return call(
            alpha_kernel, per, [by_rows(group), slab, slab, group_blocks],
            by_rows(group), result, [(group, group)] * 4, 2 * flops, "alpha_groups", {1: 0},
        )(slots, running, behind, ahead, ablocks)

    def beta_groups(slots, running, high, low, arrived):
        mask, part, buffer = arrived
        of_running = pl.BlockSpec((quarter, columns), lambda i, s: (part[0] + i, 0))
        return call(
            functools.partial(beta_kernel, [mask]), part[1] - part[0],
            [of_running, by_rows(quarter, buffer.shape[1])] + [whole(*bblocks.shape)] * 2,
            of_running, result, [(quarter, group)] * 2, flops, "beta_groups", {1: 0}, 20 * 1024 * 1024,
        )(slots, running, buffer, high, low)

    def branch(early, late):
        def body(c, near_odd, ablocks, bblocks, slots, chosen):
            sends = [(*send, whole_rows) for send in early] + [(*late, part) for part in (most_rows, last_rows)]
            pieces = [(what, part) for _, _, what, part in sends if what not in (tile, near)]
            picked = dict(zip(pieces, pick(chosen, c, pieces), strict=True)) if pieces else {}

            def start(pairs, mask, what, part):
                if what == tile:
                    x = c[part[0] * quarter : part[1] * quarter]
                else:
                    x = near_odd if what == near else picked[what, part]
                return mask, part, lax.ppermute(x, "beta", pairs)

            arrivals = [start(*send) for send in sends]
            a_behind = lax.ppermute(c, "alpha", [(i, (i + 1) % na) for i in range(na)])
            a_ahead = lax.ppermute(c, "alpha", [(i, (i - 1) % na) for i in range(na)])
            running, high, low = own_groups(slots, c, ablocks, bblocks)
            for arrived in arrivals[:-2]:
                running = beta_groups(slots, running, high, low, arrived)
            running = alpha_groups(slots, running, a_behind, a_ahead, ablocks)
            for arrived in arrivals[-2:]:
                running = beta_groups(slots, running, high, low, arrived)
            return running

        return body

    to_ahead, to_behind, far_or_end, near, tile = range(5)
    below, above = mask_of(sides=(BEHIND,)), mask_of(sides=(AHEAD,))
    even_kinds, odd_near = mask_of((EVEN,)), mask_of((ODD,), ranks=(NEAR,))
    far_or_end_kinds = mask_of((ODD,), ranks=(FAR,)) | mask_of((ENDS,))
    branches = [
        branch(
            [(odd_pairs, odd_near, near), (even_pairs, even_kinds, tile)],
            (odd_pairs + end_pairs, far_or_end_kinds, far_or_end),
        ),
        branch([(ring, below, tile)], (counter, above, tile)),
        branch([(ring, below, tile)], (counter, above, to_behind)),
        branch([(counter, above, tile)], (ring, below, to_ahead)),
        branch([(ring, below, to_ahead)], (counter, above, to_behind)),
    ]
    return lax.switch(index[0], branches, c, near_odd, ablocks, bblocks, slots, chosen)


def solution(mesh):
    in_specs = (
        P("alpha", "beta"),
        P("beta", None, None, None),
        P("alpha", None, None, None),
        P("beta", None),
        P("alpha", None),
        P("beta"),
        P("alpha"),
    )
    return jax.shard_map(
        on_device, mesh=mesh, in_specs=in_specs, out_specs=P("alpha", "beta"), check_vma=False
    )
```

```python
import functools

import jax
import jax.numpy as jnp
from jax import lax
from jax.experimental import pallas as pl
from jax.experimental.pallas import tpu as pltpu
from jax.sharding import PartitionSpec as P

VMEM_LIMIT = 56 * 1024 * 1024


def halves(x):
    high = x.astype(jnp.bfloat16)
    low = (x - high.astype(jnp.float32)).astype(jnp.bfloat16)
    return high, low


def split(x, high, low):
    height = 96

    def step(i, carry):
        rows = at(i, height)
        high[rows, :], low[rows, :] = halves(x[rows, :])
        return carry

    lax.fori_loop(0, high.shape[0] // height, step, 0)


def add_product(out, left, right, height):
    (lh, ll), (rh, rl) = left, right
    dot = functools.partial(jnp.dot, preferred_element_type=jnp.float32)

    def step(i, carry):
        rows = at(i, height)
        high, low = lh[rows, :], ll[rows, :]
        out[rows, :] += dot(high, rh[...]) + (dot(high, rl[...]) + dot(low, rh[...]))
        return carry

    lax.fori_loop(0, lh.shape[0] // height, step, 0)


def at(index, size):
    return pl.ds(pl.multiple_of(index * size, size), size)


OWN, UNUSED = 0, 13
EVEN, ODD, ENDS = range(3)
BEHIND, AHEAD = range(2)
NEAR, FAR = range(2)


def kind_of(pair, side, rank):
    return 1 + 4 * pair + 2 * side + rank


def mask_of(pairs=(EVEN, ODD, ENDS), sides=(BEHIND, AHEAD), ranks=(NEAR, FAR)):
    return sum(1 << kind_of(p, s, r) for p in pairs for s in sides for r in ranks)


def tables_kernel(owners, blinks, alinks, bcount, acount, slots, code):
    per, listed = blinks.shape
    (yn, zn), yi, zi = owners, lax.axis_index("alpha"), lax.axis_index("beta")
    first, last, even = zi == 0, zi == zn - 1, lax.rem(zi, 2) == 0
    pair_behind = jnp.where(first, ENDS, jnp.where(even, ODD, EVEN))
    pair_ahead = jnp.where(last, ENDS, jnp.where(even, EVEN, ODD))

    def where(links, count, g, l, index, n):
        slot = lax.rem(links[g, l] - index * per + per + n * per, n * per)
        return jnp.where(l < count[g], slot, -1)

    nb = fb = na = fa = jnp.int32(0)
    for g in range(per):
        for l in range(listed):
            slots[g * listed + l] = where(alinks, acount, g, l, yi, yn)
            slot = where(blinks, bcount, g, l, zi, zn)
            nb |= (slot == per - 1).astype(jnp.int32)
            fb |= (slot == per - 2).astype(jnp.int32)
            na |= (slot == 2 * per).astype(jnp.int32)
            fa |= (slot == 2 * per + 1).astype(jnp.int32)
            behind = kind_of(pair_behind, BEHIND, jnp.where(slot == per - 1, NEAR, FAR))
            ahead = kind_of(pair_ahead, AHEAD, jnp.where(slot == 2 * per, NEAR, FAR))
            kind = jnp.where(slot < per, behind, jnp.where(slot < 2 * per, OWN, ahead))
            kind = jnp.where(slot < 0, UNUSED, kind)
            slots[(per + g) * listed + l] = kind * per + lax.rem(slot + per, per)
    behind, ahead = nb + fb, na + fa
    climb = jnp.where(first, 0, behind >> 1)
    descend = jnp.where(last, 0, ahead >> 1)
    over = jnp.where(first, behind, 0)
    back = jnp.where(last, ahead, 0)
    code[0] = code[1] = climb + (descend << 6) + (over << 12) + (back << 14) + (nb << 16) + (na << 17)


def pick_kernel(chosen, *refs):
    for source, target in zip(refs[: len(refs) // 2], refs[len(refs) // 2 :], strict=True):
        target[...] = source[...]


def own_kernel(slots, tile, tile_rows, ablocks, bblocks, out, high, low, lh, ll, rh, rl):
    per, listed, group, _ = bblocks.shape
    row = pl.program_id(0)
    out[...] = jnp.zeros_like(out)

    def step(u, carry):
        t = u // 2
        g, l = t // listed, lax.rem(t, listed)
        a_slot, b_slot = slots[row * listed + l], slots[per * listed + t]
        of_alpha = lax.rem(u, 2) == 0
        in_alpha = of_alpha & (a_slot >= per) & (a_slot < 2 * per)
        in_beta = jnp.logical_not(of_alpha) & (lax.div(b_slot, per) == OWN)

        @pl.when(in_alpha)
        def _():
            split(ablocks.at[0, l], lh, ll)
            split(tile.at[at(a_slot - per, group), at(g, group)], rh, rl)

        @pl.when(jnp.logical_not(of_alpha))
        def _():
            split(bblocks.at[g, l], rh, rl)

            @pl.when(row == 0)
            def _():
                high[g, l], low[g, l] = rh[...], rl[...]

        @pl.when(in_beta)
        def _():
            split(tile_rows.at[:, at(b_slot, group)], lh, ll)

        @pl.when(in_alpha | in_beta)
        def _():
            add_product(out.at[:, at(g, group)], (lh, ll), (rh, rl), 96)

        return carry

    lax.fori_loop(0, 2 * per * listed, step, 0)


def alpha_kernel(slots, running, behind, ahead, ablocks, out, lh, ll, rh, rl):
    _, listed, group, _ = ablocks.shape
    per = behind.shape[0] // group
    row = pl.program_id(0)
    out[...] = running[...]

    def step(t, carry):
        l, g = t // per, lax.rem(t, per)
        slot = slots[row * listed + l]
        below, above = (slot >= 0) & (slot < per), slot >= 2 * per
        for inside, tile, base in ((below, behind, 0), (above, ahead, 2 * per)):

            @pl.when(inside)
            def _(tile=tile, base=base):
                split(tile.at[at(slot - base, group), at(g, group)], rh, rl)

        @pl.when((below | above) & (g == 0))
        def _():
            split(ablocks.at[0, l], lh, ll)

        @pl.when(below | above)
        def _():
            add_product(out.at[:, at(g, group)], (lh, ll), (rh, rl), 192)

        return carry

    lax.fori_loop(0, per * listed, step, 0)


def beta_kernel(masks, slots, running, *refs):
    *buffers, high, low, out, lh, ll = refs
    per, listed, group, _ = high.shape
    out[...] = running[...]

    def step(t, carry):
        g, l = t // listed, lax.rem(t, listed)
        slot = slots[per * listed + t]
        hits = []
        for mask, tile in zip(masks, buffers, strict=True):
            hits.append(((mask >> lax.div(slot, per)) & 1) == 1)

            @pl.when(hits[-1])
            def _(tile=tile):
                split(tile if tile.shape[1] == group else tile.at[:, at(lax.rem(slot, per), group)], lh, ll)

        @pl.when(functools.reduce(jnp.logical_or, hits))
        def _():
            add_product(out.at[:, at(g, group)], (lh, ll), (high.at[g, l], low.at[g, l]), lh.shape[0])

        return carry

    lax.fori_loop(0, per * listed, step, 0)


def call(kernel, grid, in_specs, out_spec, shape, scratch, flops, name, aliases, vmem=VMEM_LIMIT):
    return pl.pallas_call(
        kernel,
        grid_spec=pltpu.PrefetchScalarGridSpec(
            num_scalar_prefetch=1, grid=(grid,), in_specs=in_specs, out_specs=out_spec,
            scratch_shapes=[pltpu.VMEM(x, jnp.bfloat16) for x in scratch],
        ),
        out_shape=shape,
        input_output_aliases=aliases,
        compiler_params=pltpu.CompilerParams(vmem_limit_bytes=vmem),
        cost_estimate=pl.CostEstimate(flops=flops, bytes_accessed=16 * 1024 * 1024, transcendentals=0),
        name=name,
    )


def on_device(c, bblocks, ablocks, blinks, alinks, bcount, acount):
    rows, columns = c.shape
    per, listed, group, _ = ablocks.shape
    na, nb = lax.axis_size("alpha"), lax.axis_size("beta")
    smem = pl.BlockSpec(memory_space=pltpu.SMEM)
    slots, code = pl.pallas_call(
        functools.partial(tables_kernel, (na, nb)),
        in_specs=[smem] * 4,
        out_specs=[smem] * 2,
        out_shape=[jax.ShapeDtypeStruct((2 * per * listed,), jnp.int32), jax.ShapeDtypeStruct((2,), jnp.int32)],
        name="tables",
    )(blinks, alinks, bcount, acount)

    codes = [code] + [
        lax.ppermute(code, "beta", [(i, (i + by) % nb) for i in range(nb)]) for by in range(1, nb)
    ]
    z = lax.axis_index("beta")
    even = z % 2 == 0
    near_odd = lax.dynamic_slice_in_dim(c, jnp.where(even, 0, per - 1) * group, group, 1)
    *codes, near_odd = lax.optimization_barrier((*codes, near_odd))
    total = functools.reduce(lambda x, y: x + y, [x & 0xFFFF for x in codes])
    climb, descend = (total & 0x3F) > 0, (total & 0xFC0) > 0
    over, back = (total & 0x3000) == 0x2000, (total & 0xC000) == 0x8000
    full = (climb & back) | (descend & over) | (over & back)
    index = jnp.where(full, 1, jnp.where(over, 2, jnp.where(back, 3, jnp.where(climb | descend, 0, 4))))
    to_ahead = jnp.where((codes[nb - 1] & 0x10000) > 0, per - 1, per - 2)
    to_behind = jnp.where((codes[1] & 0x20000) > 0, 0, 1)
    far_odd = jnp.where(even, 1, per - 2)
    to_end = jnp.where(even, to_behind, to_ahead)
    chosen = jnp.stack([to_ahead, to_behind, jnp.where((z == 0) | (z == nb - 1), to_end, far_odd)])[:, 0]

    def whole(*shape):
        return pl.BlockSpec(shape, lambda i, s: (0,) * len(shape))

    def by_rows(n, width=columns):
        return pl.BlockSpec((n, width), lambda i, s: (i, 0))

    group_blocks = pl.BlockSpec((1, listed, group, group), lambda i, s: (i, 0, 0, 0))
    slab = whole(rows, columns)
    result = jax.ShapeDtypeStruct(c.shape, jnp.float32)
    half = jax.ShapeDtypeStruct(bblocks.shape, jnp.bfloat16)
    flops = 2 * rows * group * group * 3 * 3
    ring = [(i, (i + 1) % nb) for i in range(nb)]
    counter = [(j, i) for i, j in ring]
    even_pairs = [p for i in range(0, nb - 1, 2) for p in ((i, i + 1), (i + 1, i))]
    odd_pairs = [p for i in range(1, nb - 1, 2) for p in ((i, i + 1), (i + 1, i))]
    end_pairs = [(0, nb - 1), (nb - 1, 0)]

    quarter = rows // 4
    whole_rows, most_rows, last_rows = (0, 4), (0, 3), (3, 4)

    def pick(chosen, c, pieces):
        def source(what, part):
            height = (part[1] - part[0]) * quarter
            return pl.BlockSpec((height, group), lambda i, s: (part[0] * quarter // height, s[what]))

        heights = [(part[1] - part[0]) * quarter for _, part in pieces]
        return pl.pallas_call(
            pick_kernel,
            grid_spec=pltpu.PrefetchScalarGridSpec(
                num_scalar_prefetch=1,
                grid=(1,),
                in_specs=[source(*piece) for piece in pieces],
                out_specs=[whole(height, group) for height in heights],
            ),
            out_shape=[jax.ShapeDtypeStruct((height, group), c.dtype) for height in heights],
            name="pick",
        )(chosen, *[c for _ in pieces])

    def own_groups(slots, c, ablocks, bblocks):
        return call(
            own_kernel, per,
            [slab, by_rows(group), group_blocks, whole(*bblocks.shape)],
            [by_rows(group), whole(*bblocks.shape), whole(*bblocks.shape)], [result, half, half],
            [(group, group)] * 4, 2 * flops, "own_groups", {},
        )(slots, c, c, ablocks, bblocks)

    def alpha_groups(slots, running, behind, ahead, ablocks):
        return call(
            alpha_kernel, per, [by_rows(group), slab, slab, group_blocks],
            by_rows(group), result, [(group, group)] * 4, 2 * flops, "alpha_groups", {1: 0},
        )(slots, running, behind, ahead, ablocks)

    def beta_groups(slots, running, high, low, arrived):
        part, buffers = arrived[0][1], [buffer for _, _, buffer in arrived]
        of_running = pl.BlockSpec((quarter, columns), lambda i, s: (part[0] + i, 0))
        return call(
            functools.partial(beta_kernel, [mask for mask, _, _ in arrived]), part[1] - part[0],
            [of_running] + [by_rows(quarter, x.shape[1]) for x in buffers] + [whole(*bblocks.shape)] * 2,
            of_running, result, [(quarter, group)] * 2, flops, "beta_groups", {1: 0}, 24 * 1024 * 1024,
        )(slots, running, *buffers, high, low)

    def branch(early, late):
        def body(c, near_odd, ablocks, bblocks, slots, chosen):
            sends = [(*send, whole_rows) for send in early] + [(*late, part) for part in (most_rows, last_rows)]
            pieces = [(what, part) for _, _, what, part in sends if what not in (tile, near)]
            picked = dict(zip(pieces, pick(chosen, c, pieces), strict=True)) if pieces else {}

            def start(pairs, mask, what, part):
                if what == tile:
                    x = c[part[0] * quarter : part[1] * quarter]
                else:
                    x = near_odd if what == near else picked[what, part]
                return mask, part, lax.ppermute(x, "beta", pairs)

            arrivals = [start(*send) for send in sends]
            a_behind = lax.ppermute(c, "alpha", [(i, (i + 1) % na) for i in range(na)])
            a_ahead = lax.ppermute(c, "alpha", [(i, (i - 1) % na) for i in range(na)])
            running, high, low = own_groups(slots, c, ablocks, bblocks)
            running = beta_groups(slots, running, high, low, arrivals[:-2])
            running = alpha_groups(slots, running, a_behind, a_ahead, ablocks)
            for arrived in arrivals[-2:]:
                running = beta_groups(slots, running, high, low, [arrived])
            return running

        return body

    to_ahead, to_behind, far_or_end, near, tile = range(5)
    below, above = mask_of(sides=(BEHIND,)), mask_of(sides=(AHEAD,))
    even_kinds, odd_near = mask_of((EVEN,)), mask_of((ODD,), ranks=(NEAR,))
    far_or_end_kinds = mask_of((ODD,), ranks=(FAR,)) | mask_of((ENDS,))
    branches = [
        branch(
            [(odd_pairs, odd_near, near), (even_pairs, even_kinds, tile)],
            (odd_pairs + end_pairs, far_or_end_kinds, far_or_end),
        ),
        branch([(ring, below, tile)], (counter, above, tile)),
        branch([(ring, below, tile)], (counter, above, to_behind)),
        branch([(counter, above, tile)], (ring, below, to_ahead)),
        branch([(ring, below, to_ahead)], (counter, above, to_behind)),
    ]
    return lax.switch(index[0], branches, c, near_odd, ablocks, bblocks, slots, chosen)


def solution(mesh):
    in_specs = (
        P("alpha", "beta"),
        P("beta", None, None, None),
        P("alpha", None, None, None),
        P("beta", None),
        P("alpha", None),
        P("beta"),
        P("alpha"),
    )
    return jax.shard_map(
        on_device, mesh=mesh, in_specs=in_specs, out_specs=P("alpha", "beta"), check_vma=False
    )
```

```python
import functools

import jax
import jax.numpy as jnp
from jax import lax
from jax.experimental import pallas as pl
from jax.experimental.pallas import tpu as pltpu
from jax.sharding import PartitionSpec as P

VMEM_LIMIT = 56 * 1024 * 1024


def halves(x):
    high = x.astype(jnp.bfloat16)
    low = (x - high.astype(jnp.float32)).astype(jnp.bfloat16)
    return high, low


def split(x, high, low):
    height = 96

    def step(i, carry):
        rows = at(i, height)
        high[rows, :], low[rows, :] = halves(x[rows, :])
        return carry

    lax.fori_loop(0, high.shape[0] // height, step, 0)


def add_product(out, left, right, height):
    (lh, ll), (rh, rl) = left, right
    dot = functools.partial(jnp.dot, preferred_element_type=jnp.float32)

    def step(i, carry):
        rows = at(i, height)
        high, low = lh[rows, :], ll[rows, :]
        out[rows, :] += dot(high, rh[...]) + (dot(high, rl[...]) + dot(low, rh[...]))
        return carry

    lax.fori_loop(0, lh.shape[0] // height, step, 0)


def at(index, size):
    return pl.ds(pl.multiple_of(index * size, size), size)


OWN, UNUSED = 0, 13
EVEN, ODD, ENDS = range(3)
BEHIND, AHEAD = range(2)
NEAR, FAR = range(2)


def kind_of(pair, side, rank):
    return 1 + 4 * pair + 2 * side + rank


def mask_of(pairs=(EVEN, ODD, ENDS), sides=(BEHIND, AHEAD), ranks=(NEAR, FAR)):
    return sum(1 << kind_of(p, s, r) for p in pairs for s in sides for r in ranks)


def tables_kernel(owners, blinks, alinks, bcount, acount, slots, code):
    per, listed = blinks.shape
    (yn, zn), yi, zi = owners, lax.axis_index("alpha"), lax.axis_index("beta")
    first, last, even = zi == 0, zi == zn - 1, lax.rem(zi, 2) == 0
    pair_behind = jnp.where(first, ENDS, jnp.where(even, ODD, EVEN))
    pair_ahead = jnp.where(last, ENDS, jnp.where(even, EVEN, ODD))

    def where(links, count, g, l, index, n):
        slot = lax.rem(links[g, l] - index * per + per + n * per, n * per)
        return jnp.where(l < count[g], slot, -1)

    nb = fb = na = fa = jnp.int32(0)
    for g in range(per):
        for l in range(listed):
            slots[g * listed + l] = where(alinks, acount, g, l, yi, yn)
            slot = where(blinks, bcount, g, l, zi, zn)
            nb |= (slot == per - 1).astype(jnp.int32)
            fb |= (slot == per - 2).astype(jnp.int32)
            na |= (slot == 2 * per).astype(jnp.int32)
            fa |= (slot == 2 * per + 1).astype(jnp.int32)
            behind = kind_of(pair_behind, BEHIND, jnp.where(slot == per - 1, NEAR, FAR))
            ahead = kind_of(pair_ahead, AHEAD, jnp.where(slot == 2 * per, NEAR, FAR))
            kind = jnp.where(slot < per, behind, jnp.where(slot < 2 * per, OWN, ahead))
            kind = jnp.where(slot < 0, UNUSED, kind)
            slots[(per + g) * listed + l] = kind * per + lax.rem(slot + per, per)
    behind, ahead = nb + fb, na + fa
    climb = jnp.where(first, 0, behind >> 1)
    descend = jnp.where(last, 0, ahead >> 1)
    over = jnp.where(first, behind, 0)
    back = jnp.where(last, ahead, 0)
    code[0] = code[1] = climb + (descend << 6) + (over << 12) + (back << 14) + (nb << 16) + (na << 17)


def pick_kernel(chosen, *refs):
    for source, target in zip(refs[: len(refs) // 2], refs[len(refs) // 2 :], strict=True):
        target[...] = source[...]


def own_kernel(slots, tile, tile_rows, ablocks, bblocks, out, high, low, lh, ll, rh, rl):
    per, listed, group, _ = bblocks.shape
    row = pl.program_id(0)
    out[...] = jnp.zeros_like(out)

    def step(u, carry):
        t = u // 2
        g, l = t // listed, lax.rem(t, listed)
        a_slot, b_slot = slots[row * listed + l], slots[per * listed + t]
        of_alpha = lax.rem(u, 2) == 0
        in_alpha = of_alpha & (a_slot >= per) & (a_slot < 2 * per)
        in_beta = jnp.logical_not(of_alpha) & (lax.div(b_slot, per) == OWN)

        @pl.when(in_alpha)
        def _():
            split(ablocks.at[0, l], lh, ll)
            split(tile.at[at(a_slot - per, group), at(g, group)], rh, rl)

        @pl.when(jnp.logical_not(of_alpha))
        def _():
            split(bblocks.at[g, l], rh, rl)

            @pl.when(row == 0)
            def _():
                high[g, l], low[g, l] = rh[...], rl[...]

        @pl.when(in_beta)
        def _():
            split(tile_rows.at[:, at(b_slot, group)], lh, ll)

        @pl.when(in_alpha | in_beta)
        def _():
            add_product(out.at[:, at(g, group)], (lh, ll), (rh, rl), 192)

        return carry

    lax.fori_loop(0, 2 * per * listed, step, 0)


def alpha_kernel(slots, running, behind, ahead, ablocks, out, lh, ll, rh, rl):
    _, listed, group, _ = ablocks.shape
    per = behind.shape[0] // group
    row = pl.program_id(0)
    out[...] = running[...]

    def step(t, carry):
        l, g = t // per, lax.rem(t, per)
        slot = slots[row * listed + l]
        below, above = (slot >= 0) & (slot < per), slot >= 2 * per
        for inside, tile, base in ((below, behind, 0), (above, ahead, 2 * per)):

            @pl.when(inside)
            def _(tile=tile, base=base):
                split(tile.at[at(slot - base, group), at(g, group)], rh, rl)

        @pl.when((below | above) & (g == 0))
        def _():
            split(ablocks.at[0, l], lh, ll)

        @pl.when(below | above)
        def _():
            add_product(out.at[:, at(g, group)], (lh, ll), (rh, rl), lh.shape[0])

        return carry

    lax.fori_loop(0, per * listed, step, 0)


def beta_kernel(masks, slots, running, *refs):
    *buffers, high, low, out, lh, ll = refs
    per, listed, group, _ = high.shape
    out[...] = running[...]

    def step(t, carry):
        g, l = t // listed, lax.rem(t, listed)
        slot = slots[per * listed + t]
        hits = []
        for mask, tile in zip(masks, buffers, strict=True):
            hits.append(((mask >> lax.div(slot, per)) & 1) == 1)

            @pl.when(hits[-1])
            def _(tile=tile):
                split(tile if tile.shape[1] == group else tile.at[:, at(lax.rem(slot, per), group)], lh, ll)

        @pl.when(functools.reduce(jnp.logical_or, hits))
        def _():
            add_product(out.at[:, at(g, group)], (lh, ll), (high.at[g, l], low.at[g, l]), lh.shape[0])

        return carry

    lax.fori_loop(0, per * listed, step, 0)


def call(kernel, grid, in_specs, out_spec, shape, scratch, flops, name, aliases, vmem=VMEM_LIMIT):
    return pl.pallas_call(
        kernel,
        grid_spec=pltpu.PrefetchScalarGridSpec(
            num_scalar_prefetch=1, grid=(grid,), in_specs=in_specs, out_specs=out_spec,
            scratch_shapes=[pltpu.VMEM(x, jnp.bfloat16) for x in scratch],
        ),
        out_shape=shape,
        input_output_aliases=aliases,
        compiler_params=pltpu.CompilerParams(vmem_limit_bytes=vmem),
        cost_estimate=pl.CostEstimate(flops=flops, bytes_accessed=16 * 1024 * 1024, transcendentals=0),
        name=name,
    )


def on_device(c, bblocks, ablocks, blinks, alinks, bcount, acount):
    rows, columns = c.shape
    per, listed, group, _ = ablocks.shape
    na, nb = lax.axis_size("alpha"), lax.axis_size("beta")
    smem = pl.BlockSpec(memory_space=pltpu.SMEM)
    slots, code = pl.pallas_call(
        functools.partial(tables_kernel, (na, nb)),
        in_specs=[smem] * 4,
        out_specs=[smem] * 2,
        out_shape=[jax.ShapeDtypeStruct((2 * per * listed,), jnp.int32), jax.ShapeDtypeStruct((2,), jnp.int32)],
        name="tables",
    )(blinks, alinks, bcount, acount)

    codes = [code] + [
        lax.ppermute(code, "beta", [(i, (i + by) % nb) for i in range(nb)]) for by in range(1, nb)
    ]
    z = lax.axis_index("beta")
    even = z % 2 == 0
    near_odd = lax.dynamic_slice_in_dim(c, jnp.where(even, 0, per - 1) * group, group, 1)
    *codes, near_odd = lax.optimization_barrier((*codes, near_odd))
    total = functools.reduce(lambda x, y: x + y, [x & 0xFFFF for x in codes])
    climb, descend = (total & 0x3F) > 0, (total & 0xFC0) > 0
    over, back = (total & 0x3000) == 0x2000, (total & 0xC000) == 0x8000
    full = (climb & back) | (descend & over) | (over & back)
    index = jnp.where(full, 1, jnp.where(over, 2, jnp.where(back, 3, 0)))
    to_ahead = jnp.where((codes[nb - 1] & 0x10000) > 0, per - 1, per - 2)
    to_behind = jnp.where((codes[1] & 0x20000) > 0, 0, 1)
    far_odd = jnp.where(even, 1, per - 2)
    to_end = jnp.where(even, to_behind, to_ahead)
    chosen = jnp.stack([to_ahead, to_behind, jnp.where((z == 0) | (z == nb - 1), to_end, far_odd)])[:, 0]

    def whole(*shape):
        return pl.BlockSpec(shape, lambda i, s: (0,) * len(shape))

    def by_rows(n, width=columns):
        return pl.BlockSpec((n, width), lambda i, s: (i, 0))

    group_blocks = pl.BlockSpec((1, listed, group, group), lambda i, s: (i, 0, 0, 0))
    slab = whole(rows, columns)
    result = jax.ShapeDtypeStruct(c.shape, jnp.float32)
    half = jax.ShapeDtypeStruct(bblocks.shape, jnp.bfloat16)
    flops = 2 * rows * group * group * 3 * 3
    ring = [(i, (i + 1) % nb) for i in range(nb)]
    counter = [(j, i) for i, j in ring]
    even_pairs = [p for i in range(0, nb - 1, 2) for p in ((i, i + 1), (i + 1, i))]
    odd_pairs = [p for i in range(1, nb - 1, 2) for p in ((i, i + 1), (i + 1, i))]
    end_pairs = [(0, nb - 1), (nb - 1, 0)]

    quarter = rows // 4
    whole_rows, most_rows, last_rows = (0, 4), (0, 3), (3, 4)

    def pick(chosen, c, pieces):
        def source(what, part):
            height = (part[1] - part[0]) * quarter
            return pl.BlockSpec((height, group), lambda i, s: (part[0] * quarter // height, s[what]))

        heights = [(part[1] - part[0]) * quarter for _, part in pieces]
        return pl.pallas_call(
            pick_kernel,
            grid_spec=pltpu.PrefetchScalarGridSpec(
                num_scalar_prefetch=1,
                grid=(1,),
                in_specs=[source(*piece) for piece in pieces],
                out_specs=[whole(height, group) for height in heights],
            ),
            out_shape=[jax.ShapeDtypeStruct((height, group), c.dtype) for height in heights],
            name="pick",
        )(chosen, *[c for _ in pieces])

    def own_groups(slots, c, ablocks, bblocks):
        return call(
            own_kernel, per,
            [slab, by_rows(group), group_blocks, whole(*bblocks.shape)],
            [by_rows(group), whole(*bblocks.shape), whole(*bblocks.shape)], [result, half, half],
            [(group, group)] * 4, 2 * flops, "own_groups", {},
        )(slots, c, c, ablocks, bblocks)

    def alpha_groups(slots, running, behind, ahead, ablocks):
        return call(
            alpha_kernel, per, [by_rows(group), slab, slab, group_blocks],
            by_rows(group), result, [(group, group)] * 4, 2 * flops, "alpha_groups", {1: 0},
        )(slots, running, behind, ahead, ablocks)

    def beta_groups(slots, running, high, low, arrived, weight=1):
        part, buffers = arrived[0][1], [buffer for _, _, buffer in arrived]
        of_running = pl.BlockSpec((quarter, columns), lambda i, s: (part[0] + i, 0))
        return call(
            functools.partial(beta_kernel, [mask for mask, _, _ in arrived]), part[1] - part[0],
            [of_running] + [by_rows(quarter, x.shape[1]) for x in buffers] + [whole(*bblocks.shape)] * 2,
            of_running, result, [(quarter, group)] * 2, weight * flops, "beta_groups", {1: 0}, 24 * 1024 * 1024,
        )(slots, running, *buffers, high, low)

    def branch(early, late):
        def body(c, near_odd, ablocks, bblocks, slots, chosen):
            sends = [(*send, whole_rows) for send in early] + [(*late, part) for part in (most_rows, last_rows)]
            pieces = [(what, part) for _, _, what, part in sends if what not in (tile, near)]
            picked = dict(zip(pieces, pick(chosen, c, pieces), strict=True)) if pieces else {}

            def start(pairs, mask, what, part):
                if what == tile:
                    x = c[part[0] * quarter : part[1] * quarter]
                else:
                    x = near_odd if what == near else picked[what, part]
                return mask, part, lax.ppermute(x, "beta", pairs)

            arrivals = [start(*send) for send in sends]
            a_behind = lax.ppermute(c, "alpha", [(i, (i + 1) % na) for i in range(na)])
            a_ahead = lax.ppermute(c, "alpha", [(i, (i - 1) % na) for i in range(na)])
            running, high, low = own_groups(slots, c, ablocks, bblocks)
            for arrived in arrivals[:-2]:
                weight = 1 if arrived[2].shape[1] == group else 10
                running = beta_groups(slots, running, high, low, [arrived], weight)
            running = alpha_groups(slots, running, a_behind, a_ahead, ablocks)
            for arrived in arrivals[-2:]:
                running = beta_groups(slots, running, high, low, [arrived])
            return running

        return body

    to_ahead, to_behind, far_or_end, near, tile = range(5)
    below, above = mask_of(sides=(BEHIND,)), mask_of(sides=(AHEAD,))
    even_kinds, odd_near = mask_of((EVEN,)), mask_of((ODD,), ranks=(NEAR,))
    far_or_end_kinds = mask_of((ODD,), ranks=(FAR,)) | mask_of((ENDS,))
    branches = [
        branch(
            [(odd_pairs, odd_near, near), (even_pairs, even_kinds, tile)],
            (odd_pairs + end_pairs, far_or_end_kinds, far_or_end),
        ),
        branch([(ring, below, tile)], (counter, above, tile)),
        branch([(ring, below, tile)], (counter, above, to_behind)),
        branch([(counter, above, tile)], (ring, below, to_ahead)),
    ]
    return lax.switch(index[0], branches, c, near_odd, ablocks, bblocks, slots, chosen)


def solution(mesh):
    in_specs = (
        P("alpha", "beta"),
        P("beta", None, None, None),
        P("alpha", None, None, None),
        P("beta", None),
        P("alpha", None),
        P("beta"),
        P("alpha"),
    )
    return jax.shard_map(
        on_device, mesh=mesh, in_specs=in_specs, out_specs=P("alpha", "beta"), check_vma=False
    )
```

```python
import functools

import jax
import jax.numpy as jnp
from jax import lax
from jax.experimental import pallas as pl
from jax.experimental.pallas import tpu as pltpu
from jax.sharding import PartitionSpec as P

VMEM_LIMIT = 56 * 1024 * 1024


def halves(x):
    high = x.astype(jnp.bfloat16)
    low = (x - high.astype(jnp.float32)).astype(jnp.bfloat16)
    return high, low


def split(x, high, low):
    height = 96

    def step(i, carry):
        rows = at(i, height)
        high[rows, :], low[rows, :] = halves(x[rows, :])
        return carry

    lax.fori_loop(0, high.shape[0] // height, step, 0)


def add_product(out, left, right, height):
    (lh, ll), (rh, rl) = left, right
    dot = functools.partial(jnp.dot, preferred_element_type=jnp.float32)

    def step(i, carry):
        rows = at(i, height)
        high, low = lh[rows, :], ll[rows, :]
        both, twice = jnp.concatenate([high, low], axis=1), jnp.concatenate([rh[...], rh[...]], axis=0)
        out[rows, :] += dot(both, twice) + dot(high, rl[...])
        return carry

    lax.fori_loop(0, lh.shape[0] // height, step, 0)


def at(index, size):
    return pl.ds(pl.multiple_of(index * size, size), size)


OWN, UNUSED = 0, 13
EVEN, ODD, ENDS = range(3)
BEHIND, AHEAD = range(2)
NEAR, FAR = range(2)


def kind_of(pair, side, rank):
    return 1 + 4 * pair + 2 * side + rank


def mask_of(pairs=(EVEN, ODD, ENDS), sides=(BEHIND, AHEAD), ranks=(NEAR, FAR)):
    return sum(1 << kind_of(p, s, r) for p in pairs for s in sides for r in ranks)


def tables_kernel(owners, blinks, alinks, bcount, acount, slots, code):
    per, listed = blinks.shape
    (yn, zn), yi, zi = owners, lax.axis_index("alpha"), lax.axis_index("beta")
    first, last, even = zi == 0, zi == zn - 1, lax.rem(zi, 2) == 0
    pair_behind = jnp.where(first, ENDS, jnp.where(even, ODD, EVEN))
    pair_ahead = jnp.where(last, ENDS, jnp.where(even, EVEN, ODD))

    def where(links, count, g, l, index, n):
        slot = lax.rem(links[g, l] - index * per + per + n * per, n * per)
        return jnp.where(l < count[g], slot, -1)

    nb = fb = na = fa = jnp.int32(0)
    for g in range(per):
        for l in range(listed):
            slots[g * listed + l] = where(alinks, acount, g, l, yi, yn)
            slot = where(blinks, bcount, g, l, zi, zn)
            nb |= (slot == per - 1).astype(jnp.int32)
            fb |= (slot == per - 2).astype(jnp.int32)
            na |= (slot == 2 * per).astype(jnp.int32)
            fa |= (slot == 2 * per + 1).astype(jnp.int32)
            behind = kind_of(pair_behind, BEHIND, jnp.where(slot == per - 1, NEAR, FAR))
            ahead = kind_of(pair_ahead, AHEAD, jnp.where(slot == 2 * per, NEAR, FAR))
            kind = jnp.where(slot < per, behind, jnp.where(slot < 2 * per, OWN, ahead))
            kind = jnp.where(slot < 0, UNUSED, kind)
            slots[(per + g) * listed + l] = kind * per + lax.rem(slot + per, per)
    behind, ahead = nb + fb, na + fa
    climb = jnp.where(first, 0, behind >> 1)
    descend = jnp.where(last, 0, ahead >> 1)
    over = jnp.where(first, behind, 0)
    back = jnp.where(last, ahead, 0)
    code[0] = code[1] = climb + (descend << 6) + (over << 12) + (back << 14) + (nb << 16) + (na << 17)


def pick_kernel(chosen, *refs):
    for source, target in zip(refs[: len(refs) // 2], refs[len(refs) // 2 :], strict=True):
        target[...] = source[...]


def own_kernel(slots, tile, tile_rows, ablocks, bblocks, out, high, low, lh, ll, rh, rl):
    per, listed, group, _ = bblocks.shape
    row = pl.program_id(0)
    out[...] = jnp.zeros_like(out)

    def step(u, carry):
        t = u // 2
        g, l = t // listed, lax.rem(t, listed)
        a_slot, b_slot = slots[row * listed + l], slots[per * listed + t]
        of_alpha = lax.rem(u, 2) == 0
        in_alpha = of_alpha & (a_slot >= per) & (a_slot < 2 * per)
        in_beta = jnp.logical_not(of_alpha) & (lax.div(b_slot, per) == OWN)

        @pl.when(in_alpha)
        def _():
            split(ablocks.at[0, l], lh, ll)
            split(tile.at[at(a_slot - per, group), at(g, group)], rh, rl)

        @pl.when(jnp.logical_not(of_alpha))
        def _():
            split(bblocks.at[g, l], rh, rl)

            @pl.when(row == 0)
            def _():
                high[g, l], low[g, l] = rh[...], rl[...]

        @pl.when(in_beta)
        def _():
            split(tile_rows.at[:, at(b_slot, group)], lh, ll)

        @pl.when(in_alpha | in_beta)
        def _():
            add_product(out.at[:, at(g, group)], (lh, ll), (rh, rl), 192)

        return carry

    lax.fori_loop(0, 2 * per * listed, step, 0)


def alpha_kernel(slots, running, behind, ahead, ablocks, out, lh, ll, rh, rl):
    _, listed, group, _ = ablocks.shape
    per = behind.shape[0] // group
    row = pl.program_id(0)
    out[...] = running[...]

    def step(t, carry):
        l, g = t // per, lax.rem(t, per)
        slot = slots[row * listed + l]
        below, above = (slot >= 0) & (slot < per), slot >= 2 * per
        for inside, tile, base in ((below, behind, 0), (above, ahead, 2 * per)):

            @pl.when(inside)
            def _(tile=tile, base=base):
                split(tile.at[at(slot - base, group), at(g, group)], rh, rl)

        @pl.when((below | above) & (g == 0))
        def _():
            split(ablocks.at[0, l], lh, ll)

        @pl.when(below | above)
        def _():
            add_product(out.at[:, at(g, group)], (lh, ll), (rh, rl), lh.shape[0])

        return carry

    lax.fori_loop(0, per * listed, step, 0)


def beta_kernel(masks, slots, running, *refs):
    *buffers, high, low, out, lh, ll = refs
    per, listed, group, _ = high.shape
    out[...] = running[...]

    def step(t, carry):
        g, l = t // listed, lax.rem(t, listed)
        slot = slots[per * listed + t]
        hits = []
        for mask, tile in zip(masks, buffers, strict=True):
            hits.append(((mask >> lax.div(slot, per)) & 1) == 1)

            @pl.when(hits[-1])
            def _(tile=tile):
                split(tile if tile.shape[1] == group else tile.at[:, at(lax.rem(slot, per), group)], lh, ll)

        @pl.when(functools.reduce(jnp.logical_or, hits))
        def _():
            add_product(out.at[:, at(g, group)], (lh, ll), (high.at[g, l], low.at[g, l]), lh.shape[0])

        return carry

    lax.fori_loop(0, per * listed, step, 0)


def call(kernel, grid, in_specs, out_spec, shape, scratch, flops, name, aliases, vmem=VMEM_LIMIT):
    return pl.pallas_call(
        kernel,
        grid_spec=pltpu.PrefetchScalarGridSpec(
            num_scalar_prefetch=1, grid=(grid,), in_specs=in_specs, out_specs=out_spec,
            scratch_shapes=[pltpu.VMEM(x, jnp.bfloat16) for x in scratch],
        ),
        out_shape=shape,
        input_output_aliases=aliases,
        compiler_params=pltpu.CompilerParams(vmem_limit_bytes=vmem),
        cost_estimate=pl.CostEstimate(flops=flops, bytes_accessed=16 * 1024 * 1024, transcendentals=0),
        name=name,
    )


def on_device(c, bblocks, ablocks, blinks, alinks, bcount, acount):
    rows, columns = c.shape
    per, listed, group, _ = ablocks.shape
    na, nb = lax.axis_size("alpha"), lax.axis_size("beta")
    smem = pl.BlockSpec(memory_space=pltpu.SMEM)
    slots, code = pl.pallas_call(
        functools.partial(tables_kernel, (na, nb)),
        in_specs=[smem] * 4,
        out_specs=[smem] * 2,
        out_shape=[jax.ShapeDtypeStruct((2 * per * listed,), jnp.int32), jax.ShapeDtypeStruct((2,), jnp.int32)],
        name="tables",
    )(blinks, alinks, bcount, acount)

    codes = [code] + [
        lax.ppermute(code, "beta", [(i, (i + by) % nb) for i in range(nb)]) for by in range(1, nb)
    ]
    z = lax.axis_index("beta")
    even = z % 2 == 0
    near_odd = lax.dynamic_slice_in_dim(c, jnp.where(even, 0, per - 1) * group, group, 1)
    *codes, near_odd = lax.optimization_barrier((*codes, near_odd))
    total = functools.reduce(lambda x, y: x + y, [x & 0xFFFF for x in codes])
    climb, descend = (total & 0x3F) > 0, (total & 0xFC0) > 0
    over, back = (total & 0x3000) == 0x2000, (total & 0xC000) == 0x8000
    full = (climb & back) | (descend & over) | (over & back)
    index = jnp.where(full, 1, jnp.where(over, 2, jnp.where(back, 3, 0)))
    to_ahead = jnp.where((codes[nb - 1] & 0x10000) > 0, per - 1, per - 2)
    to_behind = jnp.where((codes[1] & 0x20000) > 0, 0, 1)
    far_odd = jnp.where(even, 1, per - 2)
    to_end = jnp.where(even, to_behind, to_ahead)
    chosen = jnp.stack([to_ahead, to_behind, jnp.where((z == 0) | (z == nb - 1), to_end, far_odd)])[:, 0]

    def whole(*shape):
        return pl.BlockSpec(shape, lambda i, s: (0,) * len(shape))

    def by_rows(n, width=columns):
        return pl.BlockSpec((n, width), lambda i, s: (i, 0))

    group_blocks = pl.BlockSpec((1, listed, group, group), lambda i, s: (i, 0, 0, 0))
    slab = whole(rows, columns)
    result = jax.ShapeDtypeStruct(c.shape, jnp.float32)
    half = jax.ShapeDtypeStruct(bblocks.shape, jnp.bfloat16)
    flops = 2 * rows * group * group * 3 * 3
    ring = [(i, (i + 1) % nb) for i in range(nb)]
    counter = [(j, i) for i, j in ring]
    even_pairs = [p for i in range(0, nb - 1, 2) for p in ((i, i + 1), (i + 1, i))]
    odd_pairs = [p for i in range(1, nb - 1, 2) for p in ((i, i + 1), (i + 1, i))]
    end_pairs = [(0, nb - 1), (nb - 1, 0)]

    quarter = rows // 4
    whole_rows, most_rows, last_rows = (0, 4), (0, 3), (3, 4)

    def pick(chosen, c, pieces):
        def source(what, part):
            height = (part[1] - part[0]) * quarter
            return pl.BlockSpec((height, group), lambda i, s: (part[0] * quarter // height, s[what]))

        heights = [(part[1] - part[0]) * quarter for _, part in pieces]
        return pl.pallas_call(
            pick_kernel,
            grid_spec=pltpu.PrefetchScalarGridSpec(
                num_scalar_prefetch=1,
                grid=(1,),
                in_specs=[source(*piece) for piece in pieces],
                out_specs=[whole(height, group) for height in heights],
            ),
            out_shape=[jax.ShapeDtypeStruct((height, group), c.dtype) for height in heights],
            name="pick",
        )(chosen, *[c for _ in pieces])

    def own_groups(slots, c, ablocks, bblocks):
        return call(
            own_kernel, per,
            [slab, by_rows(group), group_blocks, whole(*bblocks.shape)],
            [by_rows(group), whole(*bblocks.shape), whole(*bblocks.shape)], [result, half, half],
            [(group, group)] * 4, 2 * flops, "own_groups", {},
        )(slots, c, c, ablocks, bblocks)

    def alpha_groups(slots, running, behind, ahead, ablocks):
        return call(
            alpha_kernel, per, [by_rows(group), slab, slab, group_blocks],
            by_rows(group), result, [(group, group)] * 4, 2 * flops, "alpha_groups", {1: 0},
        )(slots, running, behind, ahead, ablocks)

    def beta_groups(slots, running, high, low, arrived, weight=1):
        part, buffers = arrived[0][1], [buffer for _, _, buffer in arrived]
        of_running = pl.BlockSpec((quarter, columns), lambda i, s: (part[0] + i, 0))
        return call(
            functools.partial(beta_kernel, [mask for mask, _, _ in arrived]), part[1] - part[0],
            [of_running] + [by_rows(quarter, x.shape[1]) for x in buffers] + [whole(*bblocks.shape)] * 2,
            of_running, result, [(quarter, group)] * 2, weight * flops, "beta_groups", {1: 0}, 24 * 1024 * 1024,
        )(slots, running, *buffers, high, low)

    def branch(early, late):
        def body(c, near_odd, ablocks, bblocks, slots, chosen):
            sends = [(*send, whole_rows) for send in early] + [(*late, part) for part in (most_rows, last_rows)]
            pieces = [(what, part) for _, _, what, part in sends if what not in (tile, near)]
            picked = dict(zip(pieces, pick(chosen, c, pieces), strict=True)) if pieces else {}

            def start(pairs, mask, what, part):
                if what == tile:
                    x = c[part[0] * quarter : part[1] * quarter]
                else:
                    x = near_odd if what == near else picked[what, part]
                return mask, part, lax.ppermute(x, "beta", pairs)

            arrivals = [start(*send) for send in sends]
            a_behind = lax.ppermute(c, "alpha", [(i, (i + 1) % na) for i in range(na)])
            a_ahead = lax.ppermute(c, "alpha", [(i, (i - 1) % na) for i in range(na)])
            running, high, low = own_groups(slots, c, ablocks, bblocks)
            for arrived in arrivals[:-2]:
                weight = 1 if arrived[2].shape[1] == group else 10
                running = beta_groups(slots, running, high, low, [arrived], weight)
            running = alpha_groups(slots, running, a_behind, a_ahead, ablocks)
            for arrived in arrivals[-2:]:
                running = beta_groups(slots, running, high, low, [arrived])
            return running

        return body

    to_ahead, to_behind, far_or_end, near, tile = range(5)
    below, above = mask_of(sides=(BEHIND,)), mask_of(sides=(AHEAD,))
    even_kinds, odd_near = mask_of((EVEN,)), mask_of((ODD,), ranks=(NEAR,))
    far_or_end_kinds = mask_of((ODD,), ranks=(FAR,)) | mask_of((ENDS,))
    branches = [
        branch(
            [(odd_pairs, odd_near, near), (even_pairs, even_kinds, tile)],
            (odd_pairs + end_pairs, far_or_end_kinds, far_or_end),
        ),
        branch([(ring, below, tile)], (counter, above, tile)),
        branch([(ring, below, tile)], (counter, above, to_behind)),
        branch([(counter, above, tile)], (ring, below, to_ahead)),
    ]
    return lax.switch(index[0], branches, c, near_odd, ablocks, bblocks, slots, chosen)


def solution(mesh):
    in_specs = (
        P("alpha", "beta"),
        P("beta", None, None, None),
        P("alpha", None, None, None),
        P("beta", None),
        P("alpha", None),
        P("beta"),
        P("alpha"),
    )
    return jax.shard_map(
        on_device, mesh=mesh, in_specs=in_specs, out_specs=P("alpha", "beta"), check_vma=False
    )
```
